512 devices in a mesh: exp: 64 (over x, z), ctx: 8 (over y, core).
Axes of the slice: x: 4, y: 4, z: 16, core: 2. Of those that a mesh axis runs over, the one named last changes fastest.
Arguments:
- y_first: bfloat16 [8192, 1024], P('exp', 'ctx'), may hold values from -6 to 6
- y_second: bfloat16 [8192, 1024], P('exp', 'ctx'), may hold values from -6 to 6
- grad_first: bfloat16 [8192, 1024], P('exp', 'ctx'), may hold values from -6 to 6
- grad_second: bfloat16 [8192, 1024], P('exp', 'ctx'), may hold values from -6 to 6
- expert_ids: int32 [8192, 6], P('exp'), may hold values from 0 to 63, all different within a row; in each aligned block of 128 rows (0 to 127, 128 to 255, ...) at most 16 rows name the same one
- gate_fixed: int32 [8192, 6], P('exp'), may hold values from 4096 to 65535
- gain_attn: float32 [1024], replicated, may hold values from 0.5 to 1.5
- gain_latent: float32 [512], replicated, may hold values from 0.5 to 1.5
- gain_moe: float32 [1024], replicated, may hold values from 0.5 to 1.5
- w_query: bfloat16 [1024, 1024], P(None, 'ctx'), may hold values from -0.1875 to 0.1875
- w_latent: bfloat16 [1024, 512], P(None, 'ctx'), may hold values from -0.1875 to 0.1875
- w_key_up: bfloat16 [512, 1024], P(None, 'ctx'), may hold values from -0.25 to 0.25
- w_value_up: bfloat16 [512, 1024], P(None, 'ctx'), may hold values from -0.25 to 0.25
- w_out: bfloat16 [1024, 1024], P('ctx'), may hold values from -0.1875 to 0.1875
- w_gate: bfloat16 [64, 1024, 1408], P('exp', None, 'ctx'), may hold values from -0.1875 to 0.1875
- w_up: bfloat16 [64, 1024, 1408], P('exp', None, 'ctx'), may hold values from -0.1875 to 0.1875
- w_down: bfloat16 [64, 1408, 1024], P('exp', 'ctx'), may hold values from -0.15625 to 0.15625
Outputs:
- first_out: bfloat16 [8192, 1024], P('exp', 'ctx')
- second_out: bfloat16 [8192, 1024], P('exp', 'ctx')
- grad_first_out: bfloat16 [8192, 1024], P('exp', 'ctx')
- grad_second_out: bfloat16 [8192, 1024], P('exp', 'ctx')
The draws below stay inside these ranges and needn't reach their ends.
Inputs may be any that keep to these rules, and one draw needn't show every extreme that they name: `expert_ids`: each row names 6 different experts. In each aligned block of 128 rows (one window, the rows of one index of exp) no expert is named by more than 16 rows, a bound that some expert reaches in every block.
All inputs are finite; a program needn't handle non-finite values.
Results may differ from the reference program's by a relative error of at most 0.025.
Values may be sent and summed in bfloat16 or wider, within the bound.
A program may use at most 64 MiB of HBM per device.

```python
import math
import jax
import jax.numpy as jnp
import numpy as np
from jax import lax

D = 1024
FF = 1408
LAT = 512
HEAD_DIM = 128
HEADS = 8
TOP = 6
EXPERTS = 64
WINDOW = 128
TOKENS = 8192
CAP = 16
N_CTX = 8


def plant(drawn, own_key, low, high):
    longest = drawn.shape.index(max(drawn.shape))
    spots = []
    for shift in (0, 1):
        where = [jax.random.randint(jax.random.fold_in(own_key, axis), (), 0, length) for axis, length in enumerate(drawn.shape)]
        where[longest] = (where[longest] + shift) % drawn.shape[longest]
        spots.append(tuple(where))
    return drawn.at[spots[0]].set(low).at[spots[1]].set(high)


def block_levels(key, extent, split, least, top_value):
    gain = 1.0
    for position, parts in split:
        steps = jax.random.uniform(jax.random.fold_in(jax.random.fold_in(key, 6), position), (parts,), jnp.float32, least / len(split), top_value / len(split))
        gain = gain * jnp.repeat(jnp.exp(steps), extent[position] // parts).reshape((-1,) + (1,) * (len(extent) - 1 - position))
    return gain


def deal_out(key, own, number, rows, count, top, limit, lean):
    order = jax.random.permutation(key, count)
    packed, usual = load_shares(count, rows * top, limit, lean, True), load_shares(count, rows * top, limit, lean, False)
    places = jnp.arange(count)

    def named(tallies, turn):
        used = int((tallies > 0).sum())
        fixed = max(1, used // 4)
        passed = fixed + (places - fixed + turn * (used - fixed)) % max(1, count - fixed)
        return jnp.zeros((count,), jnp.int32).at[order[jnp.where(places < fixed, places, passed)]].set(jnp.asarray(tallies, jnp.int32))

    tallies = jnp.where(number % 4 == 0, named(packed, number // 4), named(usual, number - number // 4 - 1))
    mixed = jax.random.permutation(jax.random.fold_in(own, 3), count)
    donor, taker = mixed[0:count // 2 * 2:2], mixed[1:count // 2 * 2:2]
    room = jnp.minimum(tallies[donor] - 1, limit - tallies[taker]) // 2
    room = jnp.where((donor == order[0]) | (taker == order[0]) | (tallies[taker] == 0), 0, jnp.maximum(room, 0))
    passed = jax.random.randint(jax.random.fold_in(own, 4), (count // 2,), 0, 1 << 20) % (room + 1)
    tallies = tallies.at[donor].add(-passed).at[taker].add(passed)
    members = jnp.searchsorted(jnp.cumsum(tallies), jnp.arange(rows * top), side="right").astype(jnp.int32)
    listing = members.reshape(top, rows).T
    listing = listing[jax.random.permutation(jax.random.fold_in(own, 1), rows)]
    turn = jax.random.randint(jax.random.fold_in(own, 2), (rows, 1), 0, top)
    return jnp.take_along_axis(listing, (jnp.arange(top)[None, :] + turn) % top, axis=1)


def load_shares(count, total, limit, slope, full):
    loads = [(1 << 20) // math.isqrt(grade ** slope) + 1 for grade in range(1, count + 1)]
    largest = limit if full else min(limit, max(-(-total // count), total * loads[0] // sum(loads)))
    least = 1 if total - largest >= count - 1 else 0
    counts, rest = [largest] + [least] * (count - 1), total - largest - least * (count - 1)
    while rest > 0:
        free = [i for i in range(1, count) if counts[i] < largest] or [i for i in range(1, count) if counts[i] < limit]
        mass, left = sum([loads[i] for i in free]), rest
        for i in free:
            addition = min(limit - counts[i], max(1, left * loads[i] // mass), rest)
            counts[i] = counts[i] + addition
            rest = rest - addition
    return np.array(counts)


def gaussian(stream_key, dims, spread, bound, split=(), dtype=jnp.bfloat16):
    result = jax.random.normal(stream_key, dims, jnp.float32) * spread
    if len(split) > 0:
        result = block_levels(stream_key, dims, split, -0.22, 0.18) * result
    return jnp.clip(result, min=-bound, max=bound).astype(dtype)


def setup_inputs(seed: int = 0) -> dict:
    keys = jax.random.split(jax.random.key(seed), 18)
    y_first = gaussian(keys[0], (TOKENS, D), 1.0, 6.0, ((0, 64), (1, 8)))
    y_second = gaussian(keys[1], (TOKENS, D), 1.0, 6.0, ((0, 64), (1, 8)))
    grad_first = gaussian(keys[2], (TOKENS, D), 1.0, 6.0, ((0, 64), (1, 8)))
    grad_second = gaussian(keys[3], (TOKENS, D), 1.0, 6.0, ((0, 64), (1, 8)))
    expert_ids_keys = jax.random.split(jax.random.fold_in(keys[4], 1), TOKENS // WINDOW)
    expert_ids_turns = jax.random.permutation(jax.random.fold_in(keys[4], 3), TOKENS // WINDOW)
    expert_ids = jax.vmap(lambda own, number: deal_out(jax.random.fold_in(keys[4], 2), own, number, WINDOW, EXPERTS, TOP, CAP, 2))(expert_ids_keys, expert_ids_turns).reshape((TOKENS, TOP))
    gate_fixed = plant(jax.random.randint(keys[5], (TOKENS, TOP), 4096, 65536), jax.random.fold_in(keys[5], 1), 4096, 65535).astype(jnp.int32)
    gain_attn = jnp.clip(1.0 + 0.1 * jax.random.normal(keys[6], (D,), jnp.float32), 0.5, 1.5)
    gain_latent = jnp.clip(1.0 + 0.1 * jax.random.normal(keys[7], (LAT,), jnp.float32), 0.5, 1.5)
    gain_moe = jnp.clip(1.0 + 0.1 * jax.random.normal(keys[8], (D,), jnp.float32), 0.5, 1.5)
    w_query = gaussian(keys[9], (D, HEADS * HEAD_DIM), D ** -0.5, 0.1875, ((1, 8),))
    w_latent = gaussian(keys[10], (D, LAT), D ** -0.5, 0.1875, ((1, 8),))
    w_key_up = gaussian(keys[11], (LAT, HEADS * HEAD_DIM), LAT ** -0.5, 0.25, ((1, 8),))
    w_value_up = gaussian(keys[12], (LAT, HEADS * HEAD_DIM), LAT ** -0.5, 0.25, ((1, 8),))
    w_out = gaussian(keys[13], (HEADS * HEAD_DIM, D), (HEADS * HEAD_DIM) ** -0.5, 0.1875, ((0, 8),))
    w_gate = gaussian(keys[14], (EXPERTS, D, FF), D ** -0.5, 0.1875, ((0, 64), (2, 8)))
    w_up = gaussian(keys[15], (EXPERTS, D, FF), D ** -0.5, 0.1875, ((0, 64), (2, 8)))
    w_down = gaussian(keys[16], (EXPERTS, FF, D), FF ** -0.5, 0.15625, ((0, 64), (1, 8)))
    return {"y_first": y_first, "y_second": y_second, "grad_first": grad_first, "grad_second": grad_second, "expert_ids": expert_ids, "gate_fixed": gate_fixed, "gain_attn": gain_attn, "gain_latent": gain_latent, "gain_moe": gain_moe, "w_query": w_query, "w_latent": w_latent, "w_key_up": w_key_up, "w_value_up": w_value_up, "w_out": w_out, "w_gate": w_gate, "w_up": w_up, "w_down": w_down}


epsilon = 1e-06
soft_limit = 5.0

def rounded(values):
    return lax.optimization_barrier(values.astype(jnp.bfloat16)).astype(jnp.float32)

def rms_scale(row_data):
    return lax.rsqrt(lax.optimization_barrier(jnp.mean(row_data * row_data, axis=-1, keepdims=True)) + epsilon)

def rms_back(row_data, gain_vec, grad_in):
    factor = rms_scale(row_data)
    weighted = gain_vec * grad_in
    inner_mean = lax.optimization_barrier(jnp.mean(weighted * row_data, axis=-1, keepdims=True))
    return factor * weighted - row_data * (factor * factor * factor) * inner_mean

def route_slots(expert_rows, expert_count):
    flat_ids = expert_rows.reshape(-1)
    labels = jnp.arange(expert_count).astype(jnp.int32)
    onehot = (flat_ids[:, None] == labels[None, :]).astype(jnp.int32)
    before = (jnp.cumsum(onehot, axis=0) - onehot).astype(jnp.int32)
    return lax.optimization_barrier(jnp.sum(before * onehot, axis=1)).astype(jnp.int32).reshape(expert_rows.shape)

def expert_pass(expert_items):
    slot_rows, slot_grads, gate_mat, up_mat, down_mat = expert_items
    slot_rows = slot_rows.reshape(-1, D).astype(jnp.float32)
    slot_grads = slot_grads.reshape(-1, D).astype(jnp.float32)
    gate_mat = gate_mat.astype(jnp.float32)
    up_mat = up_mat.astype(jnp.float32)
    down_mat = down_mat.astype(jnp.float32)
    slice_width = FF // N_CTX
    gate_proj = jnp.dot(slot_rows, gate_mat, preferred_element_type=jnp.float32)
    up_proj = jnp.dot(slot_rows, up_mat, preferred_element_type=jnp.float32)
    sigmoid_gate = jax.nn.sigmoid(gate_proj)
    hidden = rounded(gate_proj * sigmoid_gate * up_proj)
    pieces = jnp.einsum('rjf,jfd->rjd', hidden.reshape(-1, N_CTX, slice_width), down_mat.reshape(N_CTX, slice_width, D))
    expert_out = lax.optimization_barrier(jnp.sum(rounded(pieces), axis=1))
    grad_hidden = jnp.dot(slot_grads, down_mat.T, preferred_element_type=jnp.float32)
    grad_gate = rounded(grad_hidden * up_proj * sigmoid_gate * (1.0 + gate_proj * (1.0 - sigmoid_gate)))
    grad_up = rounded(grad_hidden * gate_proj * sigmoid_gate)
    back_pieces = jnp.einsum('rjf,djf->rjd', grad_gate.reshape(-1, N_CTX, slice_width), gate_mat.reshape(D, N_CTX, slice_width))
    back_pieces = back_pieces + jnp.einsum('rjf,djf->rjd', grad_up.reshape(-1, N_CTX, slice_width), up_mat.reshape(D, N_CTX, slice_width))
    expert_back = lax.optimization_barrier(jnp.sum(rounded(back_pieces), axis=1))
    return (expert_out, expert_back)

def reference(y_first, y_second, grad_first, grad_second, expert_ids, gate_fixed, gain_attn, gain_latent, gain_moe, w_query, w_latent, w_key_up, w_value_up, w_out, w_gate, w_up, w_down):
    windows = TOKENS // WINDOW
    first_in = y_first.astype(jnp.float32)
    normed = (first_in * rms_scale(first_in) * gain_moe).astype(jnp.bfloat16)
    window_ids = expert_ids.reshape(windows, WINDOW, TOP)
    slot_ids = jax.vmap(lambda part_ids: route_slots(part_ids, EXPERTS))(window_ids)
    window_index = jnp.broadcast_to(jnp.arange(windows).astype(jnp.int32)[:, None, None], window_ids.shape)
    token_index = jnp.broadcast_to(jnp.arange(TOKENS).astype(jnp.int32).reshape(windows, WINDOW)[:, :, None], window_ids.shape)
    empty_buffer = jnp.zeros((EXPERTS, windows, CAP, D), jnp.bfloat16)
    row_buffer = empty_buffer.at[window_ids, window_index, slot_ids].set(normed[token_index])
    grad_buffer = empty_buffer.at[window_ids, window_index, slot_ids].set(grad_second[token_index])
    expert_out, expert_back = lax.map(expert_pass, (row_buffer, grad_buffer, w_gate, w_up, w_down))
    expert_out = expert_out.reshape(EXPERTS, windows, CAP, D)
    expert_back = expert_back.reshape(EXPERTS, windows, CAP, D)
    weights = gate_fixed.astype(jnp.float32).reshape(windows, WINDOW, TOP) / 65536.0
    moe_out = lax.optimization_barrier(jnp.sum(weights[..., None] * expert_out[window_ids, window_index, slot_ids], axis=2)).reshape(TOKENS, D)
    grad_moe = lax.optimization_barrier(jnp.sum(weights[..., None] * expert_back[window_ids, window_index, slot_ids], axis=2)).reshape(TOKENS, D)
    second_out = (y_second.astype(jnp.float32) - moe_out).astype(jnp.bfloat16)
    total_grad = grad_first.astype(jnp.float32) + rms_back(first_in, gain_moe, grad_moe)
    grad_first_out = total_grad.astype(jnp.bfloat16)
    second = second_out.astype(jnp.float32)
    attn_in = (second * rms_scale(second) * gain_attn).astype(jnp.bfloat16)
    queries = jnp.dot(attn_in, w_query, preferred_element_type=jnp.float32).astype(jnp.bfloat16)
    latent = jnp.dot(attn_in, w_latent, preferred_element_type=jnp.float32).astype(jnp.bfloat16)
    latent_f = latent.astype(jnp.float32)
    latent_norm = (latent_f * rms_scale(latent_f) * gain_latent).astype(jnp.bfloat16)
    key_rows = jnp.dot(latent_norm, w_key_up, preferred_element_type=jnp.float32).astype(jnp.bfloat16)
    value_rows = jnp.dot(latent_norm, w_value_up, preferred_element_type=jnp.float32).astype(jnp.bfloat16)
    head_shape = (windows, WINDOW, HEADS, HEAD_DIM)
    query_heads = queries.reshape(head_shape).astype(jnp.float32)
    key_heads = key_rows.reshape(head_shape).astype(jnp.float32)
    value_heads = value_rows.reshape(head_shape).astype(jnp.float32)
    scale_factor = 1.0 / math.sqrt(HEAD_DIM)
    raw_scores = jnp.einsum('nqhk,nshk->nhqs', query_heads, key_heads) * scale_factor
    bounded = jnp.tanh(raw_scores / soft_limit)
    positions = jnp.arange(WINDOW)
    allowed = positions[None, :] <= positions[:, None]
    exp_scores = jnp.where(allowed[None, None], jnp.exp(soft_limit * bounded), 0.0)
    probs_full = exp_scores / lax.optimization_barrier(jnp.sum(exp_scores, axis=-1, keepdims=True))
    probs_low = rounded(probs_full)
    mixed_heads = jnp.einsum('nhqs,nshk->nqhk', probs_low, value_heads).astype(jnp.bfloat16)
    attn_out = jnp.dot(mixed_heads.reshape(TOKENS, HEADS * HEAD_DIM), w_out, preferred_element_type=jnp.float32)
    first_out = (first_in - attn_out).astype(jnp.bfloat16)
    grad_mixed = jnp.dot(grad_first_out, w_out.T, preferred_element_type=jnp.float32).astype(jnp.bfloat16)
    grad_heads = grad_mixed.reshape(head_shape).astype(jnp.float32)
    grad_probs = jnp.einsum('nqhk,nshk->nhqs', grad_heads, value_heads)
    row_delta = lax.optimization_barrier(jnp.sum(probs_full * grad_probs, axis=-1, keepdims=True))
    grad_scores = rounded(probs_full * (grad_probs - row_delta) * (1.0 - bounded * bounded) * scale_factor)
    grad_queries = jnp.einsum('nhqs,nshk->nqhk', grad_scores, key_heads).astype(jnp.bfloat16)
    grad_keys = jnp.einsum('nhqs,nqhk->nshk', grad_scores, query_heads).astype(jnp.bfloat16)
    grad_values = jnp.einsum('nhqs,nqhk->nshk', probs_low, grad_heads).astype(jnp.bfloat16)
    flat_width = HEADS * HEAD_DIM
    grad_latent_norm = jnp.dot(grad_keys.reshape(TOKENS, flat_width), w_key_up.T, preferred_element_type=jnp.float32)
    grad_latent_norm = grad_latent_norm + jnp.dot(grad_values.reshape(TOKENS, flat_width), w_value_up.T, preferred_element_type=jnp.float32)
    grad_latent = rms_back(latent_f, gain_latent, grad_latent_norm).astype(jnp.bfloat16)
    grad_attn_in = jnp.dot(grad_queries.reshape(TOKENS, flat_width), w_query.T, preferred_element_type=jnp.float32)
    grad_attn_in = grad_attn_in + jnp.dot(grad_latent, w_latent.T, preferred_element_type=jnp.float32)
    grad_second_out = (grad_second.astype(jnp.float32) + rms_back(second, gain_attn, grad_attn_in)).astype(jnp.bfloat16)
    return (first_out, second_out, grad_first_out, grad_second_out)
```

```python
import functools
import math

import jax
import jax.numpy as jnp
from jax import lax
from jax.experimental import pallas as pl
from jax.experimental.pallas import tpu as pltpu
from jax.sharding import PartitionSpec as P

CAP = 16
N_CTX = 8
EPS = 1e-06
LIMIT = 5.0
MESH = pl.DeviceIdType.MESH
F32 = jnp.float32
BF16 = jnp.bfloat16


def dot_nn(a, b):
    return lax.dot_general(a, b, (((1,), (0,)), ((), ())), preferred_element_type=F32)


def dot_nt(a, b):
    return lax.dot_general(a, b, (((1,), (1,)), ((), ())), preferred_element_type=F32)


def dot_tn(a, b):
    return lax.dot_general(a, b, (((0,), (0,)), ((), ())), preferred_element_type=F32)


def scale_of(v):
    return lax.rsqrt(jnp.mean(v * v, axis=-1, keepdims=True) + EPS)


def iota(shape, axis):
    return lax.broadcasted_iota(jnp.int32, shape, axis)


def wide(ref, count):
    return jnp.concatenate([ref[i] for i in range(count)], axis=1)


def kernel(
    n_x,
    n_z,
    cap,
    yf_ref,
    ys_ref,
    gf_ref,
    gs_ref,
    ids_ref,
    gate_ref,
    g_attn,
    g_lat,
    g_moe,
    wq,
    wl,
    wk,
    wv,
    wo,
    wg,
    wu,
    wd,
    first_out,
    second_out,
    gfirst_out,
    gsecond_out,
    yf_all,
    gf_all,
    gs_grp,
    ys_grp,
    wg_all,
    wu_all,
    wd_all,
    comb,
    rows_send,
    grads_send,
    rows_in,
    grads_in,
    up_keep,
    gate_keep,
    xo_send,
    xo_recv,
    out_ret,
    out_back,
    xb_send,
    xb_recv,
    bk_ret,
    bk_back,
    sec,
    gm,
    lat_all,
    ao_send,
    ao_recv,
    gff,
    lg_send,
    lg_recv,
    ia_send,
    ia_recv,
    yf_s,
    yf_r,
    gf_s,
    gf_r,
    grp_s,
    grp_r,
    w_s,
    w_r,
    disp_s,
    disp_r,
    cross_s,
    cross_r,
    ret_s,
    ret_r,
    sec_s,
    sec_r,
    gm_s,
    gm_r,
    lat_s,
    lat_r,
    ao_s,
    ao_r,
    lg_s,
    lg_r,
    ia_s,
    ia_r,
):
    n_exp = n_x * n_z
    zi_n = n_z // 4
    wins = n_x * zi_n
    me = lax.axis_index("exp")
    c = lax.axis_index("ctx")
    mx, mz = me // n_z, me % n_z
    y, k = c // 2, c % 2
    p, j = c // 4, c % 4
    q = 2 * (((y + 1) // 2) % 2) + k
    mate = c + 1 - 2 * k
    nbr = c + 2 - 4 * (y % 2)
    cross = 6 - 2 * y + k
    quarter = (mx + mz) % 4
    my_wi = mx * zi_n + mz // 4
    active = q == quarter
    qm, qk = quarter // 2, quarter % 2
    act = 2 * (p * (3 - 2 * qm) + qm) + qk
    half = pl.ds(pl.multiple_of(p * 512, 512), 512)
    other = pl.ds(pl.multiple_of((1 - p) * 512, 512), 512)

    def remote(src, dst, ssem, rsem, e, cc):
        return pltpu.make_async_remote_copy(
            src_ref=src,
            dst_ref=dst,
            send_sem=ssem,
            recv_sem=rsem,
            device_id=(e, cc),
            device_id_type=MESH,
        )

    def wait_bytes(ref, sem):
        pltpu.make_async_copy(ref, ref, sem).wait()

    def shifted(i):
        a, dx = i // n_x, i % n_x
        dz = (a % 2) * ((a + 1) // 2) + (1 - a % 2) * (n_z - a // 2)
        return ((mx + dx) % n_x) * n_z + (mz + dz) % n_z

    barrier = pltpu.get_barrier_semaphore()

    @pl.loop(1, n_exp)
    def _(i):
        pl.semaphore_signal(barrier, inc=1, device_id=(shifted(i), c), device_id_type=MESH)

    @pl.loop(1, N_CTX)
    def _(d):
        pl.semaphore_signal(barrier, inc=1, device_id=(me, (c + d) % N_CTX), device_id_type=MESH)

    yf_all[c] = yf_ref[...]
    gf_all[c] = gf_ref[...]
    gs_grp[j] = gs_ref[...]
    ys_grp[j] = ys_ref[...]
    wg_all[j] = wg[0]
    wu_all[j] = wu[0]
    wd_all[j] = wd[0]

    pl.semaphore_wait(barrier, n_exp - 1 + N_CTX - 1)

    @pl.loop(1, N_CTX)
    def _(d):
        remote(yf_all.at[c], yf_all.at[c], yf_s, yf_r, me, (c + d) % N_CTX).start()

    @pl.when(jnp.logical_not(active))
    def _():
        remote(gs_grp.at[j], gs_grp.at[j], grp_s.at[0], grp_r.at[0], me, act).start()
        remote(ys_grp.at[j], ys_grp.at[j], grp_s.at[1], grp_r.at[1], me, act).start()

    w_alls = (wg_all, wu_all, wd_all)
    j_nbr = nbr % 4

    for n, w_all in enumerate(w_alls):
        remote(w_all.at[j], w_all.at[j], w_s.at[n, 0], w_r.at[n, 0], me, nbr).start()
        remote(w_all.at[j], w_all.at[j], w_s.at[n, 1], w_r.at[n, 1], me, mate).start()

    def forward(n):
        w_all = w_alls[n]
        wait_bytes(w_all.at[j_nbr], w_r.at[n, 0])
        remote(w_all.at[j_nbr], w_all.at[j_nbr], w_s.at[n, 2], w_r.at[n, 2], me, mate).start()

    def have(n):
        w_all = w_alls[n]
        wait_bytes(w_all.at[0], w_r.at[n, 1])
        wait_bytes(w_all.at[0], w_r.at[n, 2])

    tokens = yf_ref.shape[0]

    def one_hot(hit):
        return jnp.where(hit, 1.0, 0.0).astype(BF16)

    def routes():
        expert = iota((n_exp, tokens), 0)
        named = jnp.zeros((n_exp, tokens), F32)
        gates = jnp.zeros((n_exp, tokens), F32)
        for t in range(ids_ref.shape[0]):
            hit = ids_ref[t : t + 1, :] == expert
            named = jnp.where(hit, 1.0, named)
            gates = jnp.where(hit, gate_ref[t : t + 1, :].astype(F32), gates)
        before = one_hot(iota((tokens, tokens), 0) < iota((tokens, tokens), 1))
        rank = dot_nn(named.astype(BF16), before)
        code = jnp.where(named > 0.5, rank, 255.0).astype(BF16)
        high = jnp.floor(gates * (1.0 / 256.0))
        return code, high.astype(BF16), (gates - 256.0 * high).astype(BF16)

    @pl.when(active)
    def _():
        code, _, _ = routes()
        slots = n_exp * cap
        spread = one_hot(iota((slots, n_exp), 0) // cap == iota((slots, n_exp), 1))
        place = (iota((slots, tokens), 0) % cap).astype(F32)
        chooser = one_hot(dot_nn(spread, code) == place)

        wait_bytes(yf_all.at[pl.ds(0, 7)], yf_r)
        first = wide(yf_all, 8).astype(F32)
        r = scale_of(first)
        normed = jnp.concatenate([yf_all[4 * p + i] for i in range(4)], axis=1).astype(F32)
        normed = (normed * r * g_moe[:, half]).astype(BF16)
        rows_send[...] = dot_nn(chooser, normed).astype(BF16).reshape(n_exp, cap, 512)

        @pl.loop(1, n_exp)
        def _(i):
            e = shifted(n_exp - i)
            remote(rows_send.at[e], rows_in.at[p, my_wi], disp_s.at[0], disp_r.at[0], e, c).start()

        pltpu.make_async_copy(rows_send.at[me], rows_in.at[p, my_wi], disp_r.at[0]).start()

        wait_bytes(gs_grp.at[pl.ds(0, 3)], grp_r.at[0])
        grads_send[...] = dot_nn(chooser, wide(gs_grp, 4)).astype(BF16).reshape(n_exp, cap, 512)

        @pl.loop(1, n_exp)
        def _(i):
            e = shifted(n_exp - i)
            remote(grads_send.at[e], grads_in.at[p, my_wi], disp_s.at[1], disp_r.at[1], e, c).start()

        pltpu.make_async_copy(grads_send.at[me], grads_in.at[p, my_wi], disp_r.at[1]).start()

        code, high, low = routes()
        spread = one_hot(iota((n_exp, slots), 1) // cap == iota((n_exp, slots), 0))
        place = (iota((tokens, slots), 1) % cap).astype(F32)
        taken = dot_tn(code, spread) == place
        for part, (levels, unit) in enumerate(((high, 256.0), (low, 65536.0))):
            comb[part * tokens : (part + 1) * tokens] = jnp.where(
                taken, dot_tn(levels, spread) * (1.0 / unit), 0.0
            ).astype(BF16)

    @pl.when(jnp.logical_not(active))
    def _():
        wait_bytes(yf_all.at[pl.ds(0, 7)], yf_r)

    @pl.loop(1, N_CTX)
    def _(d):
        remote(gf_all.at[c], gf_all.at[c], gf_s, gf_r, me, (c + d) % N_CTX).start()

    forward(0)
    forward(1)

    wait_bytes(rows_in.at[0], disp_r.at[0])
    remote(rows_in.at[p], rows_in.at[p], cross_s.at[0], cross_r.at[0], me, cross).start()
    forward(2)
    wait_bytes(rows_in.at[0], cross_r.at[0])
    n_rows = wins * cap
    hid = 4 * wg.shape[1]

    def both(ref):
        return jnp.concatenate([ref[0].reshape(n_rows, 512), ref[1].reshape(n_rows, 512)], axis=1)

    def weight(ref):
        return ref[...].reshape(hid, 1024)

    def weight_half(ref, cols):
        return ref[:, :, cols].reshape(hid, 512)

    have(0)
    rows = both(rows_in)
    gate_proj = dot_nt(rows, weight(wg_all))
    have(1)
    up_proj = dot_nt(rows, weight(wu_all))
    gate_keep[...] = gate_proj
    up_keep[...] = up_proj
    hidden = (gate_proj * jax.nn.sigmoid(gate_proj) * up_proj).astype(BF16)
    have(2)
    xo_send[...] = dot_nn(hidden, weight_half(wd_all, other)).astype(BF16)
    remote(xo_send, xo_recv, cross_s.at[1], cross_r.at[1], me, cross).start()
    own_out = dot_nn(hidden, weight_half(wd_all, half))

    wait_bytes(grads_in.at[0], disp_r.at[1])
    remote(grads_in.at[p], grads_in.at[p], cross_s.at[2], cross_r.at[2], me, cross).start()

    def give_back(ret, back, n):
        @pl.loop(0, wins)
        def _(i):
            wx, zi = (mx + i // zi_n) % n_x, (mz // 4 + i) % zi_n
            w = wx * n_z + (q + 4 * n_x - wx) % 4 + 4 * zi
            wi = wx * zi_n + zi

            @pl.when(w != me)
            def _():
                remote(ret.at[wi], back.at[me], ret_s.at[n], ret_r.at[n], w, c).start()

        @pl.when(active)
        def _():
            pltpu.make_async_copy(ret.at[my_wi], back.at[me], ret_r.at[n]).start()

    wait_bytes(xo_recv, cross_r.at[1])
    out_ret[...] = (own_out + xo_recv[...].astype(F32)).astype(BF16).reshape(wins, cap, 512)
    give_back(out_ret, out_back, 0)

    wait_bytes(grads_in.at[0], cross_r.at[2])
    grad_hidden = dot_nt(both(grads_in), weight(wd_all))
    gate_proj = gate_keep[...]
    sig = jax.nn.sigmoid(gate_proj)
    grad_gate = (grad_hidden * up_keep[...] * sig * (1.0 + gate_proj * (1.0 - sig))).astype(BF16)
    grad_up = (grad_hidden * gate_proj * sig).astype(BF16)
    xb_send[...] = (
        dot_nn(grad_gate, weight_half(wg_all, other)) + dot_nn(grad_up, weight_half(wu_all, other))
    ).astype(BF16)
    remote(xb_send, xb_recv, cross_s.at[3], cross_r.at[3], me, cross).start()
    own_back = dot_nn(grad_gate, weight_half(wg_all, half)) + dot_nn(grad_up, weight_half(wu_all, half))
    wait_bytes(xb_recv, cross_r.at[3])
    bk_ret[...] = (own_back + xb_recv[...].astype(F32)).astype(BF16).reshape(wins, cap, 512)
    give_back(bk_ret, bk_back, 1)

    def combined(back):
        sums = dot_nn(comb[...], back[...].reshape(n_exp * cap, 512))
        return sums[0:tokens] + sums[tokens : 2 * tokens]

    def to_all(ref, ssem, rsem):
        @pl.loop(1, N_CTX)
        def _(d):
            remote(ref.at[p], ref.at[p], ssem.at[d - 1], rsem.at[p], me, (c + d) % N_CTX).start()

    @pl.when(active)
    def _():
        wait_bytes(ys_grp.at[pl.ds(0, 3)], grp_r.at[1])
        wait_bytes(out_back, ret_r.at[0])
        sec[p] = (wide(ys_grp, 4).astype(F32) - combined(out_back)).astype(BF16)
        to_all(sec, sec_s, sec_r)

    @pl.when(jnp.logical_not(active))
    def _():
        wait_bytes(sec.at[0], sec_r.at[p])

    wait_bytes(sec.at[0], sec_r.at[1 - p])
    own_lanes = pl.ds(pl.multiple_of(j * 128, 128), 128)
    second_out[...] = sec[p, :, own_lanes]

    second = jnp.concatenate([sec[0], sec[1]], axis=1).astype(F32)
    r_second = scale_of(second)
    attn_in = (second * r_second * g_attn[...]).astype(BF16)
    queries = dot_nn(attn_in, wq[...]).astype(BF16)
    wl2 = jnp.concatenate([wl[...], wl[...]], axis=0)
    lane = iota((tokens, 128), 1)
    mine = lane // 64 == k
    lat_all[c] = jnp.where(mine, dot_nt(attn_in, wl2), 0.0).astype(BF16)

    @pl.loop(1, N_CTX)
    def _(d):
        remote(lat_all.at[c], lat_all.at[c], lat_s, lat_r, me, (c + d) % N_CTX).start()

    wait_bytes(lat_all.at[pl.ds(0, 7)], lat_r)
    latent = jnp.concatenate(
        [lat_all[2 * i].astype(F32) + lat_all[2 * i + 1].astype(F32) for i in range(4)], axis=1
    )
    r_latent = scale_of(latent)
    latent_norm = (latent * r_latent * g_lat[...]).astype(BF16)
    keys = dot_nn(latent_norm, wk[...]).astype(BF16)
    values = dot_nn(latent_norm, wv[...]).astype(BF16)
    factor = 1.0 / math.sqrt(128.0)
    bounded = jnp.tanh(dot_nt(queries, keys) * (factor / LIMIT))
    allowed = iota((tokens, tokens), 1) <= iota((tokens, tokens), 0)
    weights = jnp.where(allowed, jnp.exp(LIMIT * bounded), 0.0)
    probs = weights / jnp.sum(weights, axis=-1, keepdims=True)
    probs_low = probs.astype(BF16)
    mixed = dot_nn(probs_low, values).astype(BF16)
    attn_part = dot_nn(mixed, wo[...]).astype(BF16)
    for i in range(N_CTX):
        ao_send[i] = attn_part[:, 128 * i : 128 * i + 128]
    ao_recv[c] = ao_send[c]

    @pl.loop(1, N_CTX)
    def _(d):
        to = (c + d) % N_CTX
        remote(ao_send.at[to], ao_recv.at[c], ao_s, ao_r, me, to).start()

    @pl.when(active)
    def _():
        wait_bytes(bk_back, ret_r.at[1])
        gm[p] = combined(bk_back).astype(BF16)
        to_all(gm, gm_s, gm_r)

    wait_bytes(ao_recv.at[pl.ds(0, 7)], ao_r)
    attn_out = ao_recv[0].astype(F32)
    for i in range(1, N_CTX):
        attn_out = attn_out + ao_recv[i].astype(F32)
    first_out[...] = (yf_ref[...].astype(F32) - attn_out).astype(BF16)
    wait_bytes(gf_all.at[pl.ds(0, 7)], gf_r)

    @pl.when(jnp.logical_not(active))
    def _():
        wait_bytes(gm.at[0], gm_r.at[p])

    wait_bytes(gm.at[0], gm_r.at[1 - p])

    first = wide(yf_all, 8).astype(F32)
    r_first = scale_of(first)
    lifted = g_moe[...] * jnp.concatenate([gm[0], gm[1]], axis=1).astype(F32)
    inner = jnp.mean(lifted * first, axis=-1, keepdims=True)
    total = wide(gf_all, 8).astype(F32) + (r_first * lifted - first * (r_first * r_first * r_first) * inner)
    total = total.astype(BF16)
    for i in range(N_CTX):
        gff[i] = total[:, 128 * i : 128 * i + 128]
    gfirst_out[...] = gff[c]
    grad_mixed = dot_nt(total, wo[...]).astype(BF16)
    grad_probs = dot_nt(grad_mixed, values)
    row_delta = jnp.sum(probs * grad_probs, axis=-1, keepdims=True)
    grad_scores = (probs * (grad_probs - row_delta) * (1.0 - bounded * bounded) * factor).astype(BF16)
    grad_keys = dot_tn(grad_scores, queries).astype(BF16)
    grad_values = dot_tn(probs_low, grad_mixed).astype(BF16)
    lat_part = dot_nt(grad_keys, wk[...]) + dot_nt(grad_values, wv[...])
    stat = jnp.sum(g_lat[...] * lat_part * latent, axis=-1, keepdims=True)
    stat_high = stat.astype(BF16).astype(F32)
    stat_pair = jnp.where(lane % 2 == 0, stat_high, stat - stat_high)
    for i in range(N_CTX):
        piece = lat_part[:, 128 * (i // 2) : 128 * (i // 2) + 128]
        lg_send[i] = jnp.where(lane // 64 == i % 2, piece, stat_pair).astype(BF16)
    lg_recv[c] = lg_send[c]

    @pl.loop(1, N_CTX)
    def _(d):
        to = (c + d) % N_CTX
        remote(lg_send.at[to], lg_recv.at[c], lg_s, lg_r, me, to).start()

    grad_queries = dot_nn(grad_scores, keys).astype(BF16)
    input_part = dot_nt(grad_queries, wq[...])
    own_latent = lat_all[c].astype(F32)
    pair_gain = g_lat[:, pl.ds(pl.multiple_of((c // 2) * 128, 128), 128)]
    wait_bytes(lg_recv.at[pl.ds(0, 7)], lg_r)
    arrived = lg_recv[0].astype(F32)
    for i in range(1, N_CTX):
        arrived = arrived + lg_recv[i].astype(F32)
    lat_inner = jnp.sum(jnp.where(mine, 0.0, arrived), axis=-1, keepdims=True) * (1.0 / (32.0 * 512.0))
    grad_latent = r_latent * (pair_gain * arrived) - own_latent * (r_latent * r_latent * r_latent) * lat_inner
    grad_latent = jnp.where(mine, grad_latent, 0.0).astype(BF16)
    input_part = input_part + dot_nn(grad_latent, wl2)
    stat = jnp.sum(g_attn[...] * input_part * second, axis=-1, keepdims=True)
    stat_row = jnp.broadcast_to(stat, (tokens, 128)).T[0:8]
    stat_high = stat_row.astype(BF16).astype(F32)
    stat_rows = jnp.concatenate([stat_high, stat_row - stat_high], axis=0).astype(BF16)
    for i in range(N_CTX):
        ia_send[i, 0:tokens] = input_part[:, 128 * i : 128 * i + 128].astype(BF16)
        ia_send[i, tokens : tokens + 16] = stat_rows
    ia_recv[c] = ia_send[c]

    @pl.loop(1, N_CTX)
    def _(d):
        to = (c + d) % N_CTX
        remote(ia_send.at[to], ia_recv.at[c], ia_s, ia_r, me, to).start()

    wait_bytes(ia_recv.at[pl.ds(0, 7)], ia_r)
    arrived = ia_recv[0].astype(F32)
    for i in range(1, N_CTX):
        arrived = arrived + ia_recv[i].astype(F32)
    stat_row = arrived[tokens : tokens + 1] + arrived[tokens + 8 : tokens + 9]
    in_inner = jnp.broadcast_to(stat_row, (tokens, tokens)).T * (1.0 / 1024.0)
    own_gain = g_attn[:, pl.ds(pl.multiple_of(c * 128, 128), 128)]
    own_second = sec[p, :, own_lanes].astype(F32)
    grad_in = r_second * (own_gain * arrived[0:tokens]) - own_second * (
        r_second * r_second * r_second
    ) * in_inner
    gsecond_out[...] = (gs_ref[...].astype(F32) + grad_in).astype(BF16)

    for ref, sem in (
        (yf_all, yf_s),
        (gf_all, gf_s),
        (lat_all, lat_s),
        (ao_send, ao_s),
        (lg_send, lg_s),
        (ia_send, ia_s),
    ):
        wait_bytes(ref.at[pl.ds(0, 7)], sem)
    for n, w_all in enumerate(w_alls):
        for i in range(3):
            wait_bytes(w_all.at[0], w_s.at[n, i])
    wait_bytes(rows_in.at[0], cross_s.at[0])
    wait_bytes(xo_send, cross_s.at[1])
    wait_bytes(grads_in.at[0], cross_s.at[2])
    wait_bytes(xb_send, cross_s.at[3])

    @pl.when(active)
    def _():
        for n, ref in enumerate((rows_send, grads_send)):
            wait_bytes(ref.at[pl.ds(0, n_exp - 1)], disp_s.at[n])
        for n, ref in enumerate((out_ret, bk_ret)):
            if wins > 1:
                wait_bytes(ref.at[pl.ds(0, wins - 1)], ret_s.at[n])
        for ref, sem in ((sec, sec_s), (gm, gm_s)):
            for d in range(N_CTX - 1):
                wait_bytes(ref.at[0], sem.at[d])

    @pl.when(jnp.logical_not(active))
    def _():
        wait_bytes(gs_grp.at[0], grp_s.at[0])
        wait_bytes(ys_grp.at[0], grp_s.at[1])
        for n, ref in enumerate((out_ret, bk_ret)):
            wait_bytes(ref, ret_s.at[n])


def local(n_x, n_z, cap, *args):
    (yf, ys, gf, gs, ids, gate, ga, gl, gmo, wq, wl, wk, wv, wo, wg, wu, wd) = args
    tokens = yf.shape[0]
    n_exp = n_x * n_z
    wins = n_exp // 4
    hid = wg.shape[2]
    block = (tokens, 128)
    vmem = lambda *s: pltpu.VMEM(s, BF16)
    dma = pltpu.SemaphoreType.DMA
    one = dma(())
    out = jax.ShapeDtypeStruct(block, BF16)
    spec = pl.BlockSpec(memory_space=pltpu.VMEM)
    return pl.pallas_call(
        functools.partial(kernel, n_x, n_z, cap),
        out_shape=(out,) * 4,
        in_specs=[spec] * 17,
        out_specs=(spec,) * 4,
        scratch_shapes=[
            vmem(8, *block),
            vmem(8, *block),
            vmem(4, *block),
            vmem(4, *block),
            vmem(4, hid, 1024),
            vmem(4, hid, 1024),
            vmem(4, hid, 1024),
            vmem(2 * tokens, n_exp * cap),
            vmem(n_exp, cap, 512),
            vmem(n_exp, cap, 512),
            vmem(2, wins, cap, 512),
            vmem(2, wins, cap, 512),
            pltpu.VMEM((wins * cap, 4 * hid), F32),
            pltpu.VMEM((wins * cap, 4 * hid), F32),
            vmem(wins * cap, 512),
            vmem(wins * cap, 512),
            vmem(wins, cap, 512),
            vmem(n_exp, cap, 512),
            vmem(wins * cap, 512),
            vmem(wins * cap, 512),
            vmem(wins, cap, 512),
            vmem(n_exp, cap, 512),
            vmem(2, tokens, 512),
            vmem(2, tokens, 512),
            vmem(8, *block),
            vmem(8, *block),
            vmem(8, *block),
            vmem(8, *block),
            vmem(8, *block),
            vmem(8, *block),
            vmem(8, tokens + 16, 128),
            vmem(8, tokens + 16, 128),
            one,
            one,
            one,
            one,
            dma((2,)),
            dma((2,)),
            dma((3, 3)),
            dma((3, 3)),
            dma((2,)),
            dma((2,)),
            dma((4,)),
            dma((4,)),
            dma((2,)),
            dma((2,)),
            dma((7,)),
            dma((2,)),
            dma((7,)),
            dma((2,)),
            one,
            one,
            one,
            one,
            one,
            one,
            one,
            one,
        ],
        compiler_params=pltpu.CompilerParams(
            collective_id=0, has_side_effects=True, vmem_limit_bytes=56 * 1024 * 1024
        ),
    )(
        *(yf, ys, gf, gs, ids.T, gate.T),
        *(g.reshape(1, -1) for g in (ga, gl, gmo)),
        *(wq, wl.T, wk, wv, wo),
        *(jnp.swapaxes(w, 1, 2) for w in (wg, wu)),
        wd,
    )


def solution(mesh, n_x=4, n_z=16, cap=CAP):
    rows = P("exp", "ctx")
    placed = (
        (rows,) * 4
        + (P("exp", None),) * 2
        + (P(),) * 3
        + (P(None, "ctx"),) * 4
        + (P("ctx", None), P("exp", None, "ctx"), P("exp", None, "ctx"), P("exp", "ctx", None))
    )
    return jax.shard_map(
        functools.partial(local, n_x, n_z, cap),
        mesh=mesh,
        in_specs=placed,
        out_specs=(rows,) * 4,
        check_vma=False,
    )
```

```python
import functools
import math

import jax
import jax.numpy as jnp
from jax import lax
from jax.experimental import pallas as pl
from jax.experimental.pallas import tpu as pltpu
from jax.sharding import PartitionSpec as P

CAP = 16
N_CTX = 8
EPS = 1e-06
LIMIT = 5.0
MESH = pl.DeviceIdType.MESH
F32 = jnp.float32
BF16 = jnp.bfloat16


def dot_nn(a, b):
    return lax.dot_general(a, b, (((1,), (0,)), ((), ())), preferred_element_type=F32)


def dot_nt(a, b):
    return lax.dot_general(a, b, (((1,), (1,)), ((), ())), preferred_element_type=F32)


def dot_tn(a, b):
    return lax.dot_general(a, b, (((0,), (0,)), ((), ())), preferred_element_type=F32)


def scale_of(v):
    return lax.rsqrt(jnp.mean(v * v, axis=-1, keepdims=True) + EPS)


def iota(shape, axis):
    return lax.broadcasted_iota(jnp.int32, shape, axis)


def wide(ref, count):
    return jnp.concatenate([ref[i] for i in range(count)], axis=1)


def kernel(
    n_x,
    n_z,
    cap,
    yf_ref,
    ys_ref,
    gf_ref,
    gs_ref,
    ids_ref,
    gate_ref,
    g_attn,
    g_lat,
    g_moe,
    wq,
    wl,
    wk,
    wv,
    wo,
    wg,
    wu,
    wd,
    first_out,
    second_out,
    gfirst_out,
    gsecond_out,
    yf_all,
    gf_all,
    gs_grp,
    ys_grp,
    wg_all,
    wu_all,
    wd_all,
    chooser,
    comb,
    rows_send,
    grads_send,
    rows_in,
    grads_in,
    up_keep,
    gate_keep,
    xo_send,
    xo_recv,
    out_ret,
    out_back,
    xb_send,
    xb_recv,
    bk_ret,
    bk_back,
    sec,
    gm,
    lat_all,
    ao_send,
    ao_recv,
    gff,
    lg_send,
    lg_recv,
    ia_send,
    ia_recv,
    yf_s,
    yf_r,
    gf_s,
    gf_r,
    grp_s,
    grp_r,
    w_s,
    w_r,
    disp_s,
    disp_r,
    cross_s,
    cross_r,
    ret_s,
    ret_r,
    sec_s,
    sec_r,
    gm_s,
    gm_r,
    lat_s,
    lat_r,
    ao_s,
    ao_r,
    lg_s,
    lg_r,
    ia_s,
    ia_r,
):
    n_exp = n_x * n_z
    zi_n = n_z // 4
    wins = n_x * zi_n
    me = lax.axis_index("exp")
    c = lax.axis_index("ctx")
    mx, mz = me // n_z, me % n_z
    y, k = c // 2, c % 2
    p, j = c // 4, c % 4
    q = 2 * (((y + 1) // 2) % 2) + k
    mate = c + 1 - 2 * k
    nbr = c + 2 - 4 * (y % 2)
    cross = 6 - 2 * y + k
    quarter = (mx + mz) % 4
    my_wi = mx * zi_n + mz // 4
    active = q == quarter
    qm, qk = quarter // 2, quarter % 2
    acts = [2 * (i * (3 - 2 * qm) + qm) + qk for i in range(2)]
    act = 2 * (p * (3 - 2 * qm) + qm) + qk
    half = pl.ds(pl.multiple_of(p * 512, 512), 512)
    other = pl.ds(pl.multiple_of((1 - p) * 512, 512), 512)

    def remote(src, dst, ssem, rsem, e, cc):
        return pltpu.make_async_remote_copy(
            src_ref=src,
            dst_ref=dst,
            send_sem=ssem,
            recv_sem=rsem,
            device_id=(e, cc),
            device_id_type=MESH,
        )

    def wait_bytes(ref, sem):
        pltpu.make_async_copy(ref, ref, sem).wait()

    owed = {}

    def owe(name, ref, sem):
        owed[name] = functools.partial(wait_bytes, ref, sem)

    def settle(*names):
        for name in names:
            owed.pop(name)()

    inactive = jnp.logical_not(active)

    def shifted(i):
        a, dx = i // n_x, i % n_x
        dz = (a % 2) * ((a + 1) // 2) + (1 - a % 2) * (n_z - a // 2)
        return ((mx + dx) % n_x) * n_z + (mz + dz) % n_z

    def window(i):
        wx, zi = (mx + i // zi_n) % n_x, (mz // 4 + i) % zi_n
        return wx * n_z + (q + 4 * n_x - wx) % 4 + 4 * zi, wx * zi_n + zi

    barrier = pltpu.get_barrier_semaphore()

    @pl.loop(1, N_CTX)
    def _(d):
        pl.semaphore_signal(barrier, inc=1, device_id=(me, (c + d) % N_CTX), device_id_type=MESH)

    @pl.loop(0, wins)
    def _(i):
        w, _ = window(i)

        @pl.when(w != me)
        def _():
            pl.semaphore_signal(barrier, inc=1, device_id=(w, c), device_id_type=MESH)

    yf_all[c] = yf_ref[...]
    gf_all[c] = gf_ref[...]
    gs_grp[j] = gs_ref[...]
    ys_grp[j] = ys_ref[...]
    wg_all[j] = wg[0]
    wu_all[j] = wu[0]
    wd_all[j] = wd[0]

    @pl.when(active)
    def _():
        pl.semaphore_wait(barrier, n_exp - 1 + N_CTX - 1)

    @pl.when(inactive)
    def _():
        pl.semaphore_wait(barrier, N_CTX - 1)


    def send_first(to):
        remote(yf_all.at[c], yf_all.at[c], yf_s, yf_r, me, to).start()

    def first_here(who):
        pl.when(who)(lambda: wait_bytes(yf_all.at[pl.ds(0, 7)], yf_r))

    for to in acts:
        pl.when(to != c)(functools.partial(send_first, to))
    owed["first, handler"] = functools.partial(first_here, active)

    @pl.when(inactive)
    def _():
        remote(gs_grp.at[j], gs_grp.at[j], grp_s.at[0], grp_r.at[0], me, act).start()
        remote(ys_grp.at[j], ys_grp.at[j], grp_s.at[1], grp_r.at[1], me, act).start()

    def group_sent(ref, n):
        pl.when(inactive)(lambda: wait_bytes(ref.at[0], grp_s.at[n]))

    def group_here(ref, n):
        pl.when(active)(lambda: wait_bytes(ref.at[pl.ds(0, 3)], grp_r.at[n]))

    for n, (name, ref) in enumerate((("gs", gs_grp), ("ys", ys_grp))):
        owed[name + " sent"] = functools.partial(group_sent, ref, n)
        owed[name] = functools.partial(group_here, ref, n)

    w_alls = (wg_all, wu_all, wd_all)
    j_nbr = nbr % 4

    for n, w_all in enumerate(w_alls):
        remote(w_all.at[j], w_all.at[j], w_s.at[n, 0], w_r.at[n, 0], me, nbr).start()
        remote(w_all.at[j], w_all.at[j], w_s.at[n, 1], w_r.at[n, 1], me, mate).start()
        for i in range(2):
            owe(f"w{n}{i} sent", w_all.at[0], w_s.at[n, i])
            owe(f"w{n}{i}", w_all.at[0], w_r.at[n, i])

    def forward(n):
        w_all = w_alls[n]
        settle(f"w{n}0")
        remote(w_all.at[j_nbr], w_all.at[j_nbr], w_s.at[n, 2], w_r.at[n, 2], me, mate).start()
        owe(f"w{n}2 sent", w_all.at[0], w_s.at[n, 2])
        owe(f"w{n}2", w_all.at[0], w_r.at[n, 2])

    def have(n):
        settle(f"w{n}1", f"w{n}2")

    tokens = yf_ref.shape[0]
    slots = n_exp * cap

    def one_hot(hit):
        return jnp.where(hit, 1.0, 0.0).astype(BF16)

    def routes():
        expert = iota((n_exp, tokens), 0)
        named = jnp.zeros((n_exp, tokens), F32)
        gates = jnp.zeros((n_exp, tokens), F32)
        for t in range(ids_ref.shape[0]):
            hit = ids_ref[t : t + 1, :] == expert
            named = jnp.where(hit, 1.0, named)
            gates = jnp.where(hit, gate_ref[t : t + 1, :].astype(F32), gates)
        before = one_hot(iota((tokens, tokens), 0) < iota((tokens, tokens), 1))
        rank = dot_nn(named.astype(BF16), before)
        code = jnp.where(named > 0.5, rank, 255.0).astype(BF16)
        high = jnp.floor(gates * (1.0 / 256.0))
        return code, high.astype(BF16), (gates - 256.0 * high).astype(BF16)

    @pl.when(active)
    def _():
        code, _, _ = routes()
        spread = one_hot(iota((slots, n_exp), 0) // cap == iota((slots, n_exp), 1))
        place = (iota((slots, tokens), 0) % cap).astype(F32)
        chooser[...] = one_hot(dot_nn(spread, code) == place)

    settle("first, handler")

    def dispatch(n, send, arrive):
        @pl.loop(1, n_exp)
        def _(i):
            e = shifted(n_exp - i)
            remote(send.at[e], arrive.at[p, my_wi], disp_s.at[n], disp_r.at[n], e, c).start()

        pltpu.make_async_copy(send.at[me], arrive.at[p, my_wi], disp_r.at[n]).start()

    def dispatch_sent(ref, n):
        pl.when(active)(lambda: wait_bytes(ref.at[pl.ds(0, n_exp - 1)], disp_s.at[n]))

    @pl.when(active)
    def _():
        r = scale_of(wide(yf_all, 8).astype(F32))
        normed = jnp.concatenate([yf_all[4 * p + i] for i in range(4)], axis=1).astype(F32)
        normed = (normed * r * g_moe[:, half]).astype(BF16)
        rows_send[...] = dot_nn(chooser[...], normed).astype(BF16).reshape(n_exp, cap, 512)
        dispatch(0, rows_send, rows_in)

    owed["rows sent"] = functools.partial(dispatch_sent, rows_send, 0)
    owe("rows", rows_in.at[0], disp_r.at[0])
    @pl.when(active)
    def _():
        code, high, low = routes()
        spread = one_hot(iota((n_exp, slots), 1) // cap == iota((n_exp, slots), 0))
        place = (iota((tokens, slots), 1) % cap).astype(F32)
        taken = dot_tn(code, spread) == place
        for part, (levels, unit) in enumerate(((high, 256.0), (low, 65536.0))):
            comb[part * tokens : (part + 1) * tokens] = jnp.where(
                taken, dot_tn(levels, spread) * (1.0 / unit), 0.0
            ).astype(BF16)

    @pl.loop(1, N_CTX)
    def _(d):
        to = (c + d) % N_CTX
        pl.when((to != acts[0]) & (to != acts[1]))(functools.partial(send_first, to))
        remote(gf_all.at[c], gf_all.at[c], gf_s, gf_r, me, to).start()

    owe("first sent", yf_all.at[pl.ds(0, 7)], yf_s)
    owed["first"] = functools.partial(first_here, inactive)
    owe("gf sent", gf_all.at[pl.ds(0, 7)], gf_s)
    owe("gf", gf_all.at[pl.ds(0, 7)], gf_r)
    settle("rows")

    def to_cross(n, src, dst):
        remote(src, dst, cross_s.at[n], cross_r.at[n], me, cross).start()
        owe(f"cross{n} sent", src, cross_s.at[n])
        owe(f"cross{n}", dst, cross_r.at[n])

    to_cross(0, rows_in.at[p], rows_in.at[p])
    settle("gs")

    @pl.when(active)
    def _():
        grads_send[...] = dot_nn(chooser[...], wide(gs_grp, 4)).astype(BF16).reshape(n_exp, cap, 512)
        dispatch(1, grads_send, grads_in)

    owed["grads sent"] = functools.partial(dispatch_sent, grads_send, 1)
    owe("grads", grads_in.at[0], disp_r.at[1])

    for n in range(3):
        forward(n)
    settle("cross0")
    n_rows = wins * cap
    hid = 4 * wg.shape[1]

    def both(ref):
        return jnp.concatenate([ref[0].reshape(n_rows, 512), ref[1].reshape(n_rows, 512)], axis=1)

    def weight(ref):
        return ref[...].reshape(hid, 1024)

    def weight_half(ref, cols):
        return ref[:, :, cols].reshape(hid, 512)

    have(0)
    rows = both(rows_in)
    gate_proj = dot_nt(rows, weight(wg_all))
    have(1)
    up_proj = dot_nt(rows, weight(wu_all))
    gate_keep[...] = gate_proj
    up_keep[...] = up_proj
    hidden = (gate_proj * jax.nn.sigmoid(gate_proj) * up_proj).astype(BF16)
    have(2)
    xo_send[...] = dot_nn(hidden, weight_half(wd_all, other)).astype(BF16)
    to_cross(1, xo_send, xo_recv)
    own_out = dot_nn(hidden, weight_half(wd_all, half))

    settle("grads")
    to_cross(2, grads_in.at[p], grads_in.at[p])

    def give_back(ret, back, n):
        @pl.loop(0, wins)
        def _(i):
            w, wi = window(i)

            @pl.when(w != me)
            def _():
                remote(ret.at[wi], back.at[me], ret_s.at[n], ret_r.at[n], w, c).start()

        @pl.when(active)
        def _():
            pltpu.make_async_copy(ret.at[my_wi], back.at[me], ret_r.at[n]).start()

        def sent():
            pl.when(inactive)(lambda: wait_bytes(ret, ret_s.at[n]))
            if wins > 1:
                pl.when(active)(lambda: wait_bytes(ret.at[pl.ds(0, wins - 1)], ret_s.at[n]))

        owed[f"ret{n} sent"] = sent
        owed[f"ret{n}"] = lambda: pl.when(active)(lambda: wait_bytes(back, ret_r.at[n]))

    settle("cross1")
    out_ret[...] = (own_out + xo_recv[...].astype(F32)).astype(BF16).reshape(wins, cap, 512)
    give_back(out_ret, out_back, 0)

    settle("cross2")
    grad_hidden = dot_nt(both(grads_in), weight(wd_all))
    gate_proj = gate_keep[...]
    sig = jax.nn.sigmoid(gate_proj)
    grad_gate = (grad_hidden * up_keep[...] * sig * (1.0 + gate_proj * (1.0 - sig))).astype(BF16)
    grad_up = (grad_hidden * gate_proj * sig).astype(BF16)
    xb_send[...] = (
        dot_nn(grad_gate, weight_half(wg_all, other)) + dot_nn(grad_up, weight_half(wu_all, other))
    ).astype(BF16)
    to_cross(3, xb_send, xb_recv)
    own_back = dot_nn(grad_gate, weight_half(wg_all, half)) + dot_nn(grad_up, weight_half(wu_all, half))
    settle("cross3")
    bk_ret[...] = (own_back + xb_recv[...].astype(F32)).astype(BF16).reshape(wins, cap, 512)
    give_back(bk_ret, bk_back, 1)

    def combined(back):
        sums = dot_nn(comb[...], back[...].reshape(n_exp * cap, 512))
        return sums[0:tokens] + sums[tokens : 2 * tokens]

    def to_all(name, ref, ssem, rsem):
        @pl.when(active)
        def _():
            @pl.loop(1, N_CTX)
            def _(d):
                remote(ref.at[p], ref.at[p], ssem, rsem.at[p], me, (c + d) % N_CTX).start()

        def sent():
            pl.when(active)(lambda: wait_bytes(ref.at[pl.ds(0, 7)], ssem))

        def here():
            pl.when(inactive)(lambda: wait_bytes(ref.at[0], rsem.at[p]))
            wait_bytes(ref.at[0], rsem.at[1 - p])

        owed[name + " sent"] = sent
        owed[name] = here

    settle("ys", "ret0")

    @pl.when(active)
    def _():
        sec[p] = (wide(ys_grp, 4).astype(F32) - combined(out_back)).astype(BF16)

    to_all("sec", sec, sec_s, sec_r)
    settle("sec")
    own_lanes = pl.ds(pl.multiple_of(j * 128, 128), 128)
    second_out[...] = sec[p, :, own_lanes]

    second = jnp.concatenate([sec[0], sec[1]], axis=1).astype(F32)
    r_second = scale_of(second)
    attn_in = (second * r_second * g_attn[...]).astype(BF16)
    queries = dot_nn(attn_in, wq[...]).astype(BF16)
    wl2 = jnp.concatenate([wl[...], wl[...]], axis=0)
    lane = iota((tokens, 128), 1)
    mine = lane // 64 == k
    lat_all[c] = jnp.where(mine, dot_nt(attn_in, wl2), 0.0).astype(BF16)

    @pl.loop(1, N_CTX)
    def _(d):
        remote(lat_all.at[c], lat_all.at[c], lat_s, lat_r, me, (c + d) % N_CTX).start()

    owe("lat sent", lat_all.at[pl.ds(0, 7)], lat_s)
    owe("lat", lat_all.at[pl.ds(0, 7)], lat_r)
    settle("lat")
    latent = jnp.concatenate(
        [lat_all[2 * i].astype(F32) + lat_all[2 * i + 1].astype(F32) for i in range(4)], axis=1
    )
    r_latent = scale_of(latent)
    latent_norm = (latent * r_latent * g_lat[...]).astype(BF16)
    keys = dot_nn(latent_norm, wk[...]).astype(BF16)
    values = dot_nn(latent_norm, wv[...]).astype(BF16)
    factor = 1.0 / math.sqrt(128.0)
    bounded = jnp.tanh(dot_nt(queries, keys) * (factor / LIMIT))
    allowed = iota((tokens, tokens), 1) <= iota((tokens, tokens), 0)
    weights = jnp.where(allowed, jnp.exp(LIMIT * bounded), 0.0)
    probs = weights / jnp.sum(weights, axis=-1, keepdims=True)
    probs_low = probs.astype(BF16)
    mixed = dot_nn(probs_low, values).astype(BF16)
    attn_part = dot_nn(mixed, wo[...]).astype(BF16)
    for i in range(N_CTX):
        ao_send[i] = attn_part[:, 128 * i : 128 * i + 128]
    ao_recv[c] = ao_send[c]

    @pl.loop(1, N_CTX)
    def _(d):
        to = (c + d) % N_CTX
        remote(ao_send.at[to], ao_recv.at[c], ao_s, ao_r, me, to).start()

    settle("ret1")

    @pl.when(active)
    def _():
        gm[p] = combined(bk_back).astype(BF16)

    to_all("gm", gm, gm_s, gm_r)
    owe("ao sent", ao_recv.at[pl.ds(0, 7)], ao_s)
    owe("ao", ao_recv.at[pl.ds(0, 7)], ao_r)
    settle("ao")
    attn_out = ao_recv[0].astype(F32)
    for i in range(1, N_CTX):
        attn_out = attn_out + ao_recv[i].astype(F32)
    first_out[...] = (yf_ref[...].astype(F32) - attn_out).astype(BF16)
    settle("first", "gf", "gm")

    first = wide(yf_all, 8).astype(F32)
    r_first = scale_of(first)
    lifted = g_moe[...] * jnp.concatenate([gm[0], gm[1]], axis=1).astype(F32)
    inner = jnp.mean(lifted * first, axis=-1, keepdims=True)
    total = wide(gf_all, 8).astype(F32) + (r_first * lifted - first * (r_first * r_first * r_first) * inner)
    total = total.astype(BF16)
    for i in range(N_CTX):
        gff[i] = total[:, 128 * i : 128 * i + 128]
    gfirst_out[...] = gff[c]
    grad_mixed = dot_nt(total, wo[...]).astype(BF16)
    grad_probs = dot_nt(grad_mixed, values)
    row_delta = jnp.sum(probs * grad_probs, axis=-1, keepdims=True)
    grad_scores = (probs * (grad_probs - row_delta) * (1.0 - bounded * bounded) * factor).astype(BF16)
    grad_keys = dot_tn(grad_scores, queries).astype(BF16)
    grad_values = dot_tn(probs_low, grad_mixed).astype(BF16)
    lat_part = dot_nt(grad_keys, wk[...]) + dot_nt(grad_values, wv[...])
    stat = jnp.sum(g_lat[...] * lat_part * latent, axis=-1, keepdims=True)
    stat_high = stat.astype(BF16).astype(F32)
    stat_pair = jnp.where(lane % 2 == 0, stat_high, stat - stat_high)
    for i in range(N_CTX):
        piece = lat_part[:, 128 * (i // 2) : 128 * (i // 2) + 128]
        lg_send[i] = jnp.where(lane // 64 == i % 2, piece, stat_pair).astype(BF16)
    lg_recv[c] = lg_send[c]

    @pl.loop(1, N_CTX)
    def _(d):
        to = (c + d) % N_CTX
        remote(lg_send.at[to], lg_recv.at[c], lg_s, lg_r, me, to).start()

    grad_queries = dot_nn(grad_scores, keys).astype(BF16)
    input_part = dot_nt(grad_queries, wq[...])
    own_latent = lat_all[c].astype(F32)
    pair_gain = g_lat[:, pl.ds(pl.multiple_of((c // 2) * 128, 128), 128)]
    owe("lg sent", lg_recv.at[pl.ds(0, 7)], lg_s)
    owe("lg", lg_recv.at[pl.ds(0, 7)], lg_r)
    settle("lg")
    arrived = lg_recv[0].astype(F32)
    for i in range(1, N_CTX):
        arrived = arrived + lg_recv[i].astype(F32)
    lat_inner = jnp.sum(jnp.where(mine, 0.0, arrived), axis=-1, keepdims=True) * (1.0 / (32.0 * 512.0))
    grad_latent = r_latent * (pair_gain * arrived) - own_latent * (r_latent * r_latent * r_latent) * lat_inner
    grad_latent = jnp.where(mine, grad_latent, 0.0).astype(BF16)
    input_part = input_part + dot_nn(grad_latent, wl2)
    stat = jnp.sum(g_attn[...] * input_part * second, axis=-1, keepdims=True)
    stat_row = jnp.broadcast_to(stat, (tokens, 128)).T[0:8]
    stat_high = stat_row.astype(BF16).astype(F32)
    stat_rows = jnp.concatenate([stat_high, stat_row - stat_high], axis=0).astype(BF16)
    for i in range(N_CTX):
        ia_send[i, 0:tokens] = input_part[:, 128 * i : 128 * i + 128].astype(BF16)
        ia_send[i, tokens : tokens + 16] = stat_rows
    ia_recv[c] = ia_send[c]

    @pl.loop(1, N_CTX)
    def _(d):
        to = (c + d) % N_CTX
        remote(ia_send.at[to], ia_recv.at[c], ia_s, ia_r, me, to).start()

    owe("ia sent", ia_recv.at[pl.ds(0, 7)], ia_s)
    owe("ia", ia_recv.at[pl.ds(0, 7)], ia_r)
    settle("ia")
    arrived = ia_recv[0].astype(F32)
    for i in range(1, N_CTX):
        arrived = arrived + ia_recv[i].astype(F32)
    stat_row = arrived[tokens : tokens + 1] + arrived[tokens + 8 : tokens + 9]
    in_inner = jnp.broadcast_to(stat_row, (tokens, tokens)).T * (1.0 / 1024.0)
    own_gain = g_attn[:, pl.ds(pl.multiple_of(c * 128, 128), 128)]
    own_second = sec[p, :, own_lanes].astype(F32)
    grad_in = r_second * (own_gain * arrived[0:tokens]) - own_second * (
        r_second * r_second * r_second
    ) * in_inner
    gsecond_out[...] = (gs_ref[...].astype(F32) + grad_in).astype(BF16)

    settle(*owed)


def hand_over(*refs):
    sems = refs[8]
    copies = [pltpu.make_async_copy(refs[i], refs[4 + i], sems.at[i]) for i in range(4)]
    for copy in copies:
        copy.start()
    for copy in copies:
        copy.wait()


def local(n_x, n_z, cap, *args):
    (yf, ys, gf, gs, ids, gate, ga, gl, gmo, wq, wl, wk, wv, wo, wg, wu, wd) = args
    tokens = yf.shape[0]
    n_exp = n_x * n_z
    wins = n_exp // 4
    hid = wg.shape[2]
    block = (tokens, 128)
    vmem = lambda *s: pltpu.VMEM(s, BF16)
    dma = pltpu.SemaphoreType.DMA
    one = dma(())
    out = jax.ShapeDtypeStruct(block, BF16)
    spec = pl.BlockSpec(memory_space=pltpu.VMEM)
    results = pl.pallas_call(
        functools.partial(kernel, n_x, n_z, cap),
        out_shape=(out,) * 4,
        in_specs=[spec] * 17,
        out_specs=(spec,) * 4,
        scratch_shapes=[
            vmem(8, *block),
            vmem(8, *block),
            vmem(4, *block),
            vmem(4, *block),
            vmem(4, hid, 1024),
            vmem(4, hid, 1024),
            vmem(4, hid, 1024),
            vmem(n_exp * cap, tokens),
            vmem(2 * tokens, n_exp * cap),
            vmem(n_exp, cap, 512),
            vmem(n_exp, cap, 512),
            vmem(2, wins, cap, 512),
            vmem(2, wins, cap, 512),
            pltpu.VMEM((wins * cap, 4 * hid), F32),
            pltpu.VMEM((wins * cap, 4 * hid), F32),
            vmem(wins * cap, 512),
            vmem(wins * cap, 512),
            vmem(wins, cap, 512),
            vmem(n_exp, cap, 512),
            vmem(wins * cap, 512),
            vmem(wins * cap, 512),
            vmem(wins, cap, 512),
            vmem(n_exp, cap, 512),
            vmem(8, tokens, 512),
            vmem(8, tokens, 512),
            vmem(8, *block),
            vmem(8, *block),
            vmem(8, *block),
            vmem(8, *block),
            vmem(8, *block),
            vmem(8, *block),
            vmem(8, tokens + 16, 128),
            vmem(8, tokens + 16, 128),
            one,
            one,
            one,
            one,
            dma((2,)),
            dma((2,)),
            dma((3, 3)),
            dma((3, 3)),
            dma((2,)),
            dma((2,)),
            dma((4,)),
            dma((4,)),
            dma((2,)),
            dma((2,)),
            one,
            dma((2,)),
            one,
            dma((2,)),
            one,
            one,
            one,
            one,
            one,
            one,
            one,
            one,
        ],
        compiler_params=pltpu.CompilerParams(
            collective_id=0, has_side_effects=True, vmem_limit_bytes=56 * 1024 * 1024
        ),
    )(
        *(yf, ys, gf, gs, ids.T, gate.T),
        *(g.reshape(1, -1) for g in (ga, gl, gmo)),
        *(wq, wl.T, wk, wv, wo),
        *(jnp.swapaxes(w, 1, 2) for w in (wg, wu)),
        wd,
    )
    place = pl.BlockSpec(memory_space=pl.ANY)
    return pl.pallas_call(
        hand_over,
        out_shape=(out,) * 4,
        in_specs=[place] * 4,
        out_specs=(place,) * 4,
        scratch_shapes=[dma((4,))],
    )(*results)


def solution(mesh, n_x=4, n_z=16, cap=CAP):
    rows = P("exp", "ctx")
    placed = (
        (rows,) * 4
        + (P("exp", None),) * 2
        + (P(),) * 3
        + (P(None, "ctx"),) * 4
        + (P("ctx", None), P("exp", None, "ctx"), P("exp", None, "ctx"), P("exp", "ctx", None))
    )
    return jax.shard_map(
        functools.partial(local, n_x, n_z, cap),
        mesh=mesh,
        in_specs=placed,
        out_specs=(rows,) * 4,
        check_vma=False,
    )
```

```python
import functools
import math

import jax
import jax.numpy as jnp
from jax import lax
from jax.experimental import pallas as pl
from jax.experimental.pallas import tpu as pltpu
from jax.sharding import PartitionSpec as P

CAP = 16
N_CTX = 8
EPS = 1e-06
LIMIT = 5.0
MESH = pl.DeviceIdType.MESH
F32 = jnp.float32
BF16 = jnp.bfloat16


def dot_nn(a, b):
    return lax.dot_general(a, b, (((1,), (0,)), ((), ())), preferred_element_type=F32)


def dot_nt(a, b):
    return lax.dot_general(a, b, (((1,), (1,)), ((), ())), preferred_element_type=F32)


def dot_tn(a, b):
    return lax.dot_general(a, b, (((0,), (0,)), ((), ())), preferred_element_type=F32)


def scale_of(v):
    return lax.rsqrt(jnp.mean(v * v, axis=-1, keepdims=True) + EPS)


def iota(shape, axis):
    return lax.broadcasted_iota(jnp.int32, shape, axis)


def wide(ref, count):
    return jnp.concatenate([ref[i] for i in range(count)], axis=1)


def kernel(
    n_x,
    n_z,
    cap,
    yf_ref,
    ys_ref,
    gf_ref,
    gs_ref,
    ids_ref,
    gate_ref,
    g_attn,
    g_lat,
    g_moe,
    wq,
    wl,
    wk,
    wv,
    wo,
    wg,
    wu,
    wd,
    first_out,
    second_out,
    gfirst_out,
    gsecond_out,
    yf_all,
    gf_all,
    gs_grp,
    ys_grp,
    wg_all,
    wu_all,
    wd_all,
    chooser,
    comb,
    rows_send,
    grads_send,
    rows_in,
    grads_in,
    up_keep,
    gate_keep,
    xo_send,
    xo_recv,
    out_ret,
    out_back,
    xb_send,
    xb_recv,
    bk_ret,
    bk_back,
    sec,
    wo_split,
    wo_all,
    gp_send,
    gp_recv,
    us,
    us_in,
    lat_all,
    ao_send,
    ao_recv,
    wl_all,
    ia_send,
    ia_recv,
    yf_s,
    yf_r,
    gf_s,
    gf_r,
    grp_s,
    grp_r,
    w_s,
    w_r,
    disp_s,
    disp_r,
    cross_s,
    cross_r,
    ret_s,
    ret_r,
    sec_s,
    sec_r,
    wo_s,
    wo_r,
    gp_s,
    gp_r,
    us_s,
    us_r,
    lat_s,
    lat_r,
    ao_s,
    ao_r,
    wl_s,
    wl_r,
    ia_s,
    ia_r,
):
    n_exp = n_x * n_z
    zi_n = n_z // 4
    wins = n_x * zi_n
    me = lax.axis_index("exp")
    c = lax.axis_index("ctx")
    mx, mz = me // n_z, me % n_z
    y, k = c // 2, c % 2
    p, j = c // 4, c % 4
    q = 2 * (((y + 1) // 2) % 2) + k
    mate = c + 1 - 2 * k
    nbr = c + 2 - 4 * (y % 2)
    cross = 6 - 2 * y + k
    quarter = (mx + mz) % 4
    my_wi = mx * zi_n + mz // 4
    active = q == quarter
    qm, qk = quarter // 2, quarter % 2
    acts = [2 * (i * (3 - 2 * qm) + qm) + qk for i in range(2)]
    act = 2 * (p * (3 - 2 * qm) + qm) + qk
    half = pl.ds(pl.multiple_of(p * 512, 512), 512)
    other = pl.ds(pl.multiple_of((1 - p) * 512, 512), 512)

    def remote(src, dst, ssem, rsem, e, cc):
        return pltpu.make_async_remote_copy(
            src_ref=src,
            dst_ref=dst,
            send_sem=ssem,
            recv_sem=rsem,
            device_id=(e, cc),
            device_id_type=MESH,
        )

    def wait_bytes(ref, sem):
        pltpu.make_async_copy(ref, ref, sem).wait()

    owed = {}

    def owe(name, ref, sem):
        owed[name] = functools.partial(wait_bytes, ref, sem)

    def settle(*names):
        for name in names:
            owed.pop(name)()

    inactive = jnp.logical_not(active)

    def shifted(i):
        a, dx = i // n_x, i % n_x
        dz = (a % 2) * ((a + 1) // 2) + (1 - a % 2) * (n_z - a // 2)
        return ((mx + dx) % n_x) * n_z + (mz + dz) % n_z

    def window(i):
        wx, zi = (mx + i % n_x) % n_x, (mz // 4 + 2 + i // n_x) % zi_n
        return wx * n_z + (q + 4 * n_x - wx) % 4 + 4 * zi, wx * zi_n + zi

    barrier = pltpu.get_barrier_semaphore()

    @pl.loop(1, N_CTX)
    def _(d):
        pl.semaphore_signal(barrier, inc=1, device_id=(me, (c + d) % N_CTX), device_id_type=MESH)

    @pl.loop(0, wins)
    def _(i):
        w, _ = window(i)

        @pl.when(w != me)
        def _():
            pl.semaphore_signal(barrier, inc=1, device_id=(w, c), device_id_type=MESH)

    yf_all[c] = yf_ref[...]
    gf_all[c] = gf_ref[...]
    gs_grp[j] = gs_ref[...]
    ys_grp[j] = ys_ref[...]
    wg_all[j] = wg[0]
    wu_all[j] = wu[0]
    wd_all[j] = wd[0]
    wl_all[c] = wl[...]

    @pl.when(active)
    def _():
        pl.semaphore_wait(barrier, n_exp - 1 + N_CTX - 1)

    @pl.when(inactive)
    def _():
        pl.semaphore_wait(barrier, N_CTX - 1)


    def send_first(to):
        remote(yf_all.at[c], yf_all.at[c], yf_s, yf_r, me, to).start()

    def first_here(who):
        pl.when(who)(lambda: wait_bytes(yf_all.at[pl.ds(0, 7)], yf_r))

    for to in acts:
        pl.when(to != c)(functools.partial(send_first, to))
    owed["first, handler"] = functools.partial(first_here, active)

    @pl.when(inactive)
    def _():
        remote(gs_grp.at[j], gs_grp.at[j], grp_s.at[0], grp_r.at[0], me, act).start()
        remote(ys_grp.at[j], ys_grp.at[j], grp_s.at[1], grp_r.at[1], me, act).start()

    def group_sent(ref, n):
        pl.when(inactive)(lambda: wait_bytes(ref.at[0], grp_s.at[n]))

    def group_here(ref, n):
        pl.when(active)(lambda: wait_bytes(ref.at[pl.ds(0, 3)], grp_r.at[n]))

    for n, (name, ref) in enumerate((("gs", gs_grp), ("ys", ys_grp))):
        owed[name + " sent"] = functools.partial(group_sent, ref, n)
        owed[name] = functools.partial(group_here, ref, n)

    w_alls = (wg_all, wu_all, wd_all)
    j_nbr = nbr % 4

    for n, w_all in enumerate(w_alls):
        remote(w_all.at[j], w_all.at[j], w_s.at[n, 0], w_r.at[n, 0], me, nbr).start()
        remote(w_all.at[j], w_all.at[j], w_s.at[n, 1], w_r.at[n, 1], me, mate).start()
        for i in range(2):
            owe(f"w{n}{i} sent", w_all.at[0], w_s.at[n, i])
            owe(f"w{n}{i}", w_all.at[0], w_r.at[n, i])

    @pl.loop(1, 4)
    def _(d):
        remote(wl_all.at[c], wl_all.at[c], wl_s.at[0], wl_r.at[0], me, (c + 2 * d) % N_CTX).start()

    remote(wl_all.at[c], wl_all.at[c], wl_s.at[0], wl_r.at[1], me, mate).start()
    owe("wl sent", wl_all.at[pl.ds(0, 4)], wl_s.at[0])
    owe("wl, far", wl_all.at[pl.ds(0, 3)], wl_r.at[0])
    owe("wl, mate", wl_all.at[0], wl_r.at[1])

    def forward(n):
        w_all = w_alls[n]
        settle(f"w{n}0")
        remote(w_all.at[j_nbr], w_all.at[j_nbr], w_s.at[n, 2], w_r.at[n, 2], me, mate).start()
        owe(f"w{n}2 sent", w_all.at[0], w_s.at[n, 2])
        owe(f"w{n}2", w_all.at[0], w_r.at[n, 2])

    def have(n):
        settle(f"w{n}1", f"w{n}2")

    tokens = yf_ref.shape[0]
    slots = n_exp * cap

    def stat_rows(stat):
        row = jnp.broadcast_to(stat, (tokens, 128)).T[0:8]
        high = row.astype(BF16).astype(F32)
        return jnp.concatenate([high, row - high], axis=0).astype(BF16)

    def stat_column(arrived, at):
        row = arrived[at : at + 1] + arrived[at + 8 : at + 9]
        return jnp.broadcast_to(row, (tokens, tokens)).T

    def one_hot(hit):
        return jnp.where(hit, 1.0, 0.0).astype(BF16)

    def routes():
        expert = iota((n_exp, tokens), 0)
        named = jnp.zeros((n_exp, tokens), F32)
        gates = jnp.zeros((n_exp, tokens), F32)
        for t in range(ids_ref.shape[0]):
            hit = ids_ref[t : t + 1, :] == expert
            named = jnp.where(hit, 1.0, named)
            gates = jnp.where(hit, gate_ref[t : t + 1, :].astype(F32), gates)
        before = one_hot(iota((tokens, tokens), 0) < iota((tokens, tokens), 1))
        rank = dot_nn(named.astype(BF16), before)
        code = jnp.where(named > 0.5, rank, 255.0).astype(BF16)
        high = jnp.floor(gates * (1.0 / 256.0))
        return code, high.astype(BF16), (gates - 256.0 * high).astype(BF16)

    @pl.when(active)
    def _():
        code, _, _ = routes()
        spread = one_hot(iota((slots, n_exp), 0) // cap == iota((slots, n_exp), 1))
        place = (iota((slots, tokens), 0) % cap).astype(F32)
        chooser[...] = one_hot(dot_nn(spread, code) == place)

    settle("first, handler")

    def dispatch(n, send, arrive):
        @pl.loop(1, n_exp)
        def _(i):
            e = shifted(n_exp - i)
            remote(send.at[e], arrive.at[p, my_wi], disp_s.at[n], disp_r.at[n], e, c).start()

        pltpu.make_async_copy(send.at[me], arrive.at[p, my_wi], disp_r.at[n]).start()

    def dispatch_sent(ref, n):
        pl.when(active)(lambda: wait_bytes(ref.at[pl.ds(0, n_exp - 1)], disp_s.at[n]))

    @pl.when(active)
    def _():
        r = scale_of(wide(yf_all, 8).astype(F32))
        normed = jnp.concatenate([yf_all[4 * p + i] for i in range(4)], axis=1).astype(F32)
        normed = (normed * r * g_moe[:, half]).astype(BF16)
        rows_send[...] = dot_nn(chooser[...], normed).astype(BF16).reshape(n_exp, cap, 512)
        dispatch(0, rows_send, rows_in)

    owed["rows sent"] = functools.partial(dispatch_sent, rows_send, 0)
    owe("rows", rows_in.at[0], disp_r.at[0])
    @pl.when(active)
    def _():
        code, high, low = routes()
        spread = one_hot(iota((n_exp, slots), 1) // cap == iota((n_exp, slots), 0))
        place = (iota((tokens, slots), 1) % cap).astype(F32)
        taken = dot_tn(code, spread) == place
        for part, (levels, unit) in enumerate(((high, 256.0), (low, 65536.0))):
            comb[part * tokens : (part + 1) * tokens] = jnp.where(
                taken, dot_tn(levels, spread) * (1.0 / unit), 0.0
            ).astype(BF16)

    @pl.loop(1, N_CTX)
    def _(d):
        to = (c + d) % N_CTX
        pl.when((to != acts[0]) & (to != acts[1]))(functools.partial(send_first, to))
        remote(gf_all.at[c], gf_all.at[c], gf_s, gf_r, me, to).start()

    owe("first sent", yf_all.at[pl.ds(0, 7)], yf_s)
    owed["first"] = functools.partial(first_here, inactive)
    owe("gf sent", gf_all.at[pl.ds(0, 7)], gf_s)
    owe("gf", gf_all.at[pl.ds(0, 7)], gf_r)
    settle("rows")

    def to_cross(n, src, dst):
        remote(src, dst, cross_s.at[n], cross_r.at[n], me, cross).start()
        owe(f"cross{n} sent", src, cross_s.at[n])
        owe(f"cross{n}", dst, cross_r.at[n])

    to_cross(0, rows_in.at[p], rows_in.at[p])
    settle("gs")

    @pl.when(active)
    def _():
        grads_send[...] = dot_nn(chooser[...], wide(gs_grp, 4)).astype(BF16).reshape(n_exp, cap, 512)
        dispatch(1, grads_send, grads_in)

    owed["grads sent"] = functools.partial(dispatch_sent, grads_send, 1)
    owe("grads", grads_in.at[0], disp_r.at[1])

    for n in range(3):
        forward(n)
    settle("wl, far")

    @pl.loop(1, 4)
    def _(d):
        slot = (c + 2 * d) % N_CTX
        remote(wl_all.at[slot], wl_all.at[slot], wl_s.at[1], wl_r.at[2], me, mate).start()

    owe("wl forwarded", wl_all.at[pl.ds(0, 3)], wl_s.at[1])
    owe("wl, mate's far", wl_all.at[pl.ds(0, 3)], wl_r.at[2])

    settle("cross0")
    n_rows = wins * cap
    hid = 4 * wg.shape[1]

    def both(ref):
        return jnp.concatenate([ref[0].reshape(n_rows, 512), ref[1].reshape(n_rows, 512)], axis=1)

    def weight(ref):
        return ref[...].reshape(hid, 1024)

    def weight_half(ref, cols):
        return ref[:, :, cols].reshape(hid, 512)

    have(0)
    rows = both(rows_in)
    gate_proj = dot_nt(rows, weight(wg_all))
    have(1)
    up_proj = dot_nt(rows, weight(wu_all))
    gate_keep[...] = gate_proj
    up_keep[...] = up_proj
    hidden = (gate_proj * jax.nn.sigmoid(gate_proj) * up_proj).astype(BF16)
    have(2)
    xo_send[...] = dot_nn(hidden, weight_half(wd_all, other)).astype(BF16)
    to_cross(1, xo_send, xo_recv)
    own_out = dot_nn(hidden, weight_half(wd_all, half))

    settle("grads")
    to_cross(2, grads_in.at[p], grads_in.at[p])

    def give_back(ret, back, n):
        @pl.loop(0, wins)
        def _(i):
            w, wi = window(i)

            @pl.when(w != me)
            def _():
                remote(ret.at[wi], back.at[me], ret_s.at[n], ret_r.at[n], w, c).start()

        @pl.when(active)
        def _():
            pltpu.make_async_copy(ret.at[my_wi], back.at[me], ret_r.at[n]).start()

        def sent():
            pl.when(inactive)(lambda: wait_bytes(ret, ret_s.at[n]))
            if wins > 1:
                pl.when(active)(lambda: wait_bytes(ret.at[pl.ds(0, wins - 1)], ret_s.at[n]))

        owed[f"ret{n} sent"] = sent
        owed[f"ret{n}"] = lambda: pl.when(active)(lambda: wait_bytes(back, ret_r.at[n]))

    settle("cross1")
    out_ret[...] = (own_out + xo_recv[...].astype(F32)).astype(BF16).reshape(wins, cap, 512)
    give_back(out_ret, out_back, 0)

    for i in range(2):
        wo_split[i] = wo[:, 512 * i : 512 * i + 512]
    wo_all[c] = wo_split[p]

    def send_wo(i):
        remote(wo_split.at[i], wo_all.at[c], wo_s, wo_r, me, acts[i]).start()

    def wo_sent():
        pl.when(inactive)(lambda: wait_bytes(wo_split, wo_s))
        pl.when(active)(lambda: wait_bytes(wo_split.at[0], wo_s))

    for i in range(2):
        pl.when(acts[i] != c)(functools.partial(send_wo, i))
    owed["wo sent"] = wo_sent
    owed["wo"] = lambda: pl.when(active)(lambda: wait_bytes(wo_all.at[pl.ds(0, 7)], wo_r))
    settle("cross2")
    grad_hidden = dot_nt(both(grads_in), weight(wd_all))
    gate_proj = gate_keep[...]
    sig = jax.nn.sigmoid(gate_proj)
    grad_gate = (grad_hidden * up_keep[...] * sig * (1.0 + gate_proj * (1.0 - sig))).astype(BF16)
    grad_up = (grad_hidden * gate_proj * sig).astype(BF16)
    xb_send[...] = (
        dot_nn(grad_gate, weight_half(wg_all, other)) + dot_nn(grad_up, weight_half(wu_all, other))
    ).astype(BF16)
    to_cross(3, xb_send, xb_recv)
    own_back = dot_nn(grad_gate, weight_half(wg_all, half)) + dot_nn(grad_up, weight_half(wu_all, half))
    settle("cross3")
    bk_ret[...] = (own_back + xb_recv[...].astype(F32)).astype(BF16).reshape(wins, cap, 512)
    give_back(bk_ret, bk_back, 1)
    def combined(back):
        sums = dot_nn(comb[...], back[...].reshape(n_exp * cap, 512))
        return sums[0:tokens] + sums[tokens : 2 * tokens]

    def to_all(name, ref, ssem, rsem):
        @pl.when(active)
        def _():
            @pl.loop(1, N_CTX)
            def _(d):
                remote(ref.at[p], ref.at[p], ssem, rsem.at[p], me, (c + d) % N_CTX).start()

        def sent():
            pl.when(active)(lambda: wait_bytes(ref.at[pl.ds(0, 7)], ssem))

        def here():
            pl.when(inactive)(lambda: wait_bytes(ref.at[0], rsem.at[p]))
            wait_bytes(ref.at[0], rsem.at[1 - p])

        owed[name + " sent"] = sent
        owed[name] = here

    settle("ys", "ret0")

    @pl.when(active)
    def _():
        sec[p] = (wide(ys_grp, 4).astype(F32) - combined(out_back)).astype(BF16)

    to_all("sec", sec, sec_s, sec_r)
    settle("sec")
    own_lanes = pl.ds(pl.multiple_of(j * 128, 128), 128)
    second_out[...] = sec[p, :, own_lanes]

    second = jnp.concatenate([sec[0], sec[1]], axis=1).astype(F32)
    r_second = scale_of(second)
    attn_in = (second * r_second * g_attn[...]).astype(BF16)
    queries = dot_nn(attn_in, wq[...]).astype(BF16)
    wl2 = jnp.concatenate([wl[...], wl[...]], axis=0)
    lane = iota((tokens, 128), 1)
    mine = lane // 64 == k
    lat_all[c] = jnp.where(mine, dot_nt(attn_in, wl2), 0.0).astype(BF16)

    @pl.loop(1, N_CTX)
    def _(d):
        remote(lat_all.at[c], lat_all.at[c], lat_s, lat_r, me, (c + d) % N_CTX).start()

    owe("lat sent", lat_all.at[pl.ds(0, 7)], lat_s)
    owe("lat", lat_all.at[pl.ds(0, 7)], lat_r)
    settle("lat")
    latent = jnp.concatenate(
        [lat_all[2 * i].astype(F32) + lat_all[2 * i + 1].astype(F32) for i in range(4)], axis=1
    )
    r_latent = scale_of(latent)
    latent_norm = (latent * r_latent * g_lat[...]).astype(BF16)
    keys = dot_nn(latent_norm, wk[...]).astype(BF16)
    values = dot_nn(latent_norm, wv[...]).astype(BF16)
    factor = 1.0 / math.sqrt(128.0)
    bounded = jnp.tanh(dot_nt(queries, keys) * (factor / LIMIT))
    allowed = iota((tokens, tokens), 1) <= iota((tokens, tokens), 0)
    weights = jnp.where(allowed, jnp.exp(LIMIT * bounded), 0.0)
    probs = weights / jnp.sum(weights, axis=-1, keepdims=True)
    probs_low = probs.astype(BF16)
    mixed = dot_nn(probs_low, values).astype(BF16)
    attn_part = dot_nn(mixed, wo[...]).astype(BF16)
    for i in range(N_CTX):
        ao_send[i] = attn_part[:, 128 * i : 128 * i + 128]
    ao_recv[c] = ao_send[c]

    @pl.loop(1, N_CTX)
    def _(d):
        to = (c + d) % N_CTX
        remote(ao_send.at[to], ao_recv.at[c], ao_s, ao_r, me, to).start()

    owe("ao sent", ao_recv.at[pl.ds(0, 7)], ao_s)
    owe("ao", ao_recv.at[pl.ds(0, 7)], ao_r)
    settle("first", "gf")
    first = wide(yf_all, 8).astype(F32)
    r_first = scale_of(first)
    turned = dot_nt((first * (r_first * r_first * r_first)).astype(BF16), wo[...])

    settle("wl, mate", "wl, mate's far")
    own_cols = pl.ds(pl.multiple_of(c * 128, 128), 128)
    latent_cube = (latent * (r_latent * r_latent * r_latent)).astype(BF16)
    project = wl_all[...].reshape(512, 1024)
    own_turn = dot_nn(latent_cube, wl_all[:, :, own_cols].reshape(512, 128))
    turn_stat = jnp.sum(g_attn[...] * dot_nn(latent_cube, project) * second, axis=-1, keepdims=True)

    settle("ret1", "wo")

    @pl.when(active)
    def _():
        grad = combined(bk_back)
        lifted = g_moe[:, half] * grad
        own_first = jnp.concatenate([yf_all[4 * p + i] for i in range(4)], axis=1).astype(F32)
        own_grad = jnp.concatenate([gf_all[4 * p + i] for i in range(4)], axis=1).astype(F32)
        part = dot_nt((own_grad + r_first * lifted).astype(BF16), wo_all[...].reshape(1024, 512))
        inner_rows = stat_rows(jnp.sum(lifted * own_first, axis=-1, keepdims=True))
        for i in range(N_CTX):
            gp_send[i, 0:tokens] = part[:, 128 * i : 128 * i + 128].astype(BF16)
            gp_send[i, tokens : tokens + 16] = inner_rows
        gp_recv[p] = gp_send[c]

        @pl.loop(1, N_CTX)
        def _(d):
            to = (c + d) % N_CTX
            remote(gp_send.at[to], gp_recv.at[p], gp_s, gp_r.at[p], me, to).start()

        for i in range(4):
            us[i] = grad[:, 128 * i : 128 * i + 128].astype(BF16)
        us_in[...] = us[j]

        @pl.loop(1, 4)
        def _(d):
            to = (j + d) % 4
            remote(us.at[to], us_in, us_s, us_r, me, 4 * p + to).start()

    def parts_sent():
        @pl.when(active)
        def _():
            wait_bytes(gp_send.at[pl.ds(0, 7)], gp_s)
            wait_bytes(us.at[pl.ds(0, 3)], us_s)

    def parts_here():
        pl.when(inactive)(lambda: wait_bytes(gp_recv.at[0], gp_r.at[p]))
        wait_bytes(gp_recv.at[0], gp_r.at[1 - p])

    owed["parts sent"] = parts_sent
    owed["parts"] = parts_here
    owed["us"] = lambda: pl.when(inactive)(lambda: wait_bytes(us_in, us_r))

    settle("ao")
    attn_out = ao_recv[0].astype(F32)
    for i in range(1, N_CTX):
        attn_out = attn_out + ao_recv[i].astype(F32)
    first_out[...] = (yf_ref[...].astype(F32) - attn_out).astype(BF16)

    settle("parts")
    arrived = gp_recv[0].astype(F32) + gp_recv[1].astype(F32)
    first_inner = stat_column(arrived, tokens) * (1.0 / 1024.0)
    grad_mixed = (arrived[0:tokens] - first_inner * turned).astype(BF16)
    grad_probs = dot_nt(grad_mixed, values)
    row_delta = jnp.sum(probs * grad_probs, axis=-1, keepdims=True)
    grad_scores = (probs * (grad_probs - row_delta) * (1.0 - bounded * bounded) * factor).astype(BF16)
    grad_keys = dot_tn(grad_scores, queries).astype(BF16)
    grad_values = dot_tn(probs_low, grad_mixed).astype(BF16)
    lat_part = dot_nt(grad_keys, wk[...]) + dot_nt(grad_values, wv[...])
    lifted = g_lat[...] * lat_part
    grad_queries = dot_nn(grad_scores, keys).astype(BF16)
    input_part = dot_nt(grad_queries, wq[...]) + dot_nn((r_latent * lifted).astype(BF16), project)
    lat_stat = stat_rows(jnp.sum(lifted * latent, axis=-1, keepdims=True))
    stat = jnp.sum(g_attn[...] * input_part * second, axis=-1, keepdims=True)
    in_stat = stat_rows(stat)
    for i in range(N_CTX):
        ia_send[i, 0:tokens] = input_part[:, 128 * i : 128 * i + 128].astype(BF16)
        ia_send[i, tokens : tokens + 16] = in_stat
        ia_send[i, tokens + 16 : tokens + 32] = lat_stat
    ia_recv[c] = ia_send[c]

    @pl.loop(1, N_CTX)
    def _(d):
        to = (c + d) % N_CTX
        remote(ia_send.at[to], ia_recv.at[c], ia_s, ia_r, me, to).start()

    settle("us")
    moe_gain = g_moe[:, own_cols]
    grad_first = r_first * (moe_gain * us_in[...].astype(F32)) - yf_ref[...].astype(F32) * (
        r_first * r_first * r_first
    ) * first_inner
    gfirst_out[...] = (gf_ref[...].astype(F32) + grad_first).astype(BF16)
    owe("ia sent", ia_recv.at[pl.ds(0, 7)], ia_s)
    owe("ia", ia_recv.at[pl.ds(0, 7)], ia_r)
    settle("ia")
    arrived = ia_recv[0].astype(F32)
    for i in range(1, N_CTX):
        arrived = arrived + ia_recv[i].astype(F32)
    lat_inner = stat_column(arrived, tokens + 16) * (1.0 / 512.0)
    in_inner = (stat_column(arrived, tokens) - lat_inner * turn_stat) * (1.0 / 1024.0)
    own_gain = g_attn[:, own_cols]
    own_second = sec[p, :, own_lanes].astype(F32)
    grad_in = r_second * (own_gain * (arrived[0:tokens] - lat_inner * own_turn)) - own_second * (
        r_second * r_second * r_second
    ) * in_inner
    gsecond_out[...] = (gs_ref[...].astype(F32) + grad_in).astype(BF16)

    settle(*owed)


def hand_over(*refs):
    for i in range(4):
        refs[4 + i][...] = refs[i][...]


def local(n_x, n_z, cap, *args):
    (yf, ys, gf, gs, ids, gate, ga, gl, gmo, wq, wl, wk, wv, wo, wg, wu, wd) = args
    tokens = yf.shape[0]
    n_exp = n_x * n_z
    wins = n_exp // 4
    hid = wg.shape[2]
    block = (tokens, 128)
    vmem = lambda *s: pltpu.VMEM(s, BF16)
    dma = pltpu.SemaphoreType.DMA
    one = dma(())
    out = jax.ShapeDtypeStruct(block, BF16)
    spec = pl.BlockSpec(memory_space=pltpu.VMEM)
    results = pl.pallas_call(
        functools.partial(kernel, n_x, n_z, cap),
        out_shape=(out,) * 4,
        in_specs=[spec] * 17,
        out_specs=(spec,) * 4,
        scratch_shapes=[
            vmem(8, *block),
            vmem(8, *block),
            vmem(4, *block),
            vmem(4, *block),
            vmem(4, hid, 1024),
            vmem(4, hid, 1024),
            vmem(4, hid, 1024),
            vmem(n_exp * cap, tokens),
            vmem(2 * tokens, n_exp * cap),
            vmem(n_exp, cap, 512),
            vmem(n_exp, cap, 512),
            vmem(2, wins, cap, 512),
            vmem(2, wins, cap, 512),
            pltpu.VMEM((wins * cap, 4 * hid), F32),
            pltpu.VMEM((wins * cap, 4 * hid), F32),
            vmem(wins * cap, 512),
            vmem(wins * cap, 512),
            vmem(wins, cap, 512),
            vmem(n_exp, cap, 512),
            vmem(wins * cap, 512),
            vmem(wins * cap, 512),
            vmem(wins, cap, 512),
            vmem(n_exp, cap, 512),
            vmem(8, tokens, 512),
            vmem(2, 128, 512),
            vmem(8, 128, 512),
            vmem(8, tokens + 16, 128),
            vmem(2, tokens + 16, 128),
            vmem(4, *block),
            vmem(*block),
            vmem(8, *block),
            vmem(8, *block),
            vmem(8, *block),
            vmem(8, 64, 1024),
            vmem(8, tokens + 32, 128),
            vmem(8, tokens + 32, 128),
            one,
            one,
            one,
            one,
            dma((2,)),
            dma((2,)),
            dma((3, 3)),
            dma((3, 3)),
            dma((2,)),
            dma((2,)),
            dma((4,)),
            dma((4,)),
            dma((2,)),
            dma((2,)),
            one,
            dma((2,)),
            one,
            one,
            one,
            dma((2,)),
            one,
            one,
            one,
            one,
            one,
            one,
            dma((2,)),
            dma((3,)),
            one,
            one,
        ],
        compiler_params=pltpu.CompilerParams(
            collective_id=0, has_side_effects=True, vmem_limit_bytes=56 * 1024 * 1024
        ),
    )(
        *(yf, ys, gf, gs, ids.T, gate.T),
        *(g.reshape(1, -1) for g in (ga, gl, gmo)),
        *(wq, wl.T, wk, wv, wo),
        *(jnp.swapaxes(w, 1, 2) for w in (wg, wu)),
        wd,
    )
    return pl.pallas_call(
        hand_over, out_shape=(out,) * 4, in_specs=[spec] * 4, out_specs=(spec,) * 4
    )(*results)


def solution(mesh, n_x=4, n_z=16, cap=CAP):
    rows = P("exp", "ctx")
    placed = (
        (rows,) * 4
        + (P("exp", None),) * 2
        + (P(),) * 3
        + (P(None, "ctx"),) * 4
        + (P("ctx", None), P("exp", None, "ctx"), P("exp", None, "ctx"), P("exp", "ctx", None))
    )
    return jax.shard_map(
        functools.partial(local, n_x, n_z, cap),
        mesh=mesh,
        in_specs=placed,
        out_specs=(rows,) * 4,
        check_vma=False,
    )
```

```python
import functools
import math

import jax
import jax.numpy as jnp
from jax import lax
from jax.experimental import pallas as pl
from jax.experimental.pallas import tpu as pltpu
from jax.sharding import PartitionSpec as P

CAP = 16
N_CTX = 8
EPS = 1e-06
LIMIT = 5.0
MESH = pl.DeviceIdType.MESH
F32 = jnp.float32
BF16 = jnp.bfloat16


def dot_nn(a, b):
    return lax.dot_general(a, b, (((1,), (0,)), ((), ())), preferred_element_type=F32)


def dot_nt(a, b):
    return lax.dot_general(a, b, (((1,), (1,)), ((), ())), preferred_element_type=F32)


def dot_tn(a, b):
    return lax.dot_general(a, b, (((0,), (0,)), ((), ())), preferred_element_type=F32)


def scale_of(v):
    return lax.rsqrt(jnp.mean(v * v, axis=-1, keepdims=True) + EPS)


def iota(shape, axis):
    return lax.broadcasted_iota(jnp.int32, shape, axis)


def wide(ref, count):
    return jnp.concatenate([ref[i] for i in range(count)], axis=1)


def kernel(
    n_x,
    n_z,
    cap,
    yf_ref,
    ys_ref,
    gf_ref,
    gs_ref,
    ids_ref,
    gate_ref,
    g_attn,
    g_lat,
    g_moe,
    wq,
    wl,
    wk,
    wv,
    wo,
    wg,
    wu,
    wd,
    first_out,
    second_out,
    gfirst_out,
    gsecond_out,
    yf_all,
    gf_all,
    gs_grp,
    ys_grp,
    wg_all,
    wu_all,
    wd_all,
    chooser,
    comb,
    rows_send,
    grads_send,
    rows_in,
    grads_in,
    up_keep,
    gate_keep,
    xo_send,
    xo_recv,
    out_ret,
    out_back,
    xb_send,
    xb_recv,
    bk_ret,
    bk_back,
    sec,
    wo_split,
    wo_all,
    gp_send,
    gp_recv,
    us,
    us_in,
    lat_all,
    ao_send,
    ao_recv,
    wl_all,
    ia_send,
    ia_recv,
    yf_s,
    yf_r,
    gf_s,
    gf_r,
    grp_s,
    grp_r,
    w_s,
    w_r,
    disp_s,
    disp_r,
    cross_s,
    cross_r,
    ret_s,
    ret_r,
    sec_s,
    sec_r,
    wo_s,
    wo_r,
    gp_s,
    gp_r,
    us_s,
    us_r,
    lat_s,
    lat_r,
    ao_s,
    ao_r,
    wl_s,
    wl_r,
    ia_s,
    ia_r,
):
    n_exp = n_x * n_z
    zi_n = n_z // 4
    wins = n_x * zi_n
    me = lax.axis_index("exp")
    c = lax.axis_index("ctx")
    mx, mz = me // n_z, me % n_z
    y, k = c // 2, c % 2
    p, j = c // 4, c % 4
    q = 2 * (((y + 1) // 2) % 2) + k
    mate = c + 1 - 2 * k
    nbr = c + 2 - 4 * (y % 2)
    cross = 6 - 2 * y + k
    quarter = (mx + mz) % 4
    my_wi = mx * zi_n + mz // 4
    active = q == quarter
    qm, qk = quarter // 2, quarter % 2
    acts = [2 * (i * (3 - 2 * qm) + qm) + qk for i in range(2)]
    act = 2 * (p * (3 - 2 * qm) + qm) + qk
    half = pl.ds(pl.multiple_of(p * 512, 512), 512)
    other = pl.ds(pl.multiple_of((1 - p) * 512, 512), 512)

    def remote(src, dst, ssem, rsem, e, cc):
        return pltpu.make_async_remote_copy(
            src_ref=src,
            dst_ref=dst,
            send_sem=ssem,
            recv_sem=rsem,
            device_id=(e, cc),
            device_id_type=MESH,
        )

    def wait_bytes(ref, sem):
        pltpu.make_async_copy(ref, ref, sem).wait()

    owed = {}

    def owe(name, ref, sem):
        owed[name] = functools.partial(wait_bytes, ref, sem)

    def settle(*names):
        for name in names:
            owed.pop(name)()

    inactive = jnp.logical_not(active)

    def shifted(i):
        a, dx = i // n_x, i % n_x
        dz = (a % 2) * ((a + 1) // 2) + (1 - a % 2) * (n_z - a // 2)
        return ((mx + dx) % n_x) * n_z + (mz + dz) % n_z

    def window(i):
        wx, zi = (mx + i % n_x) % n_x, (mz // 4 + 2 + i // n_x) % zi_n
        return wx * n_z + (q + 4 * n_x - wx) % 4 + 4 * zi, wx * zi_n + zi

    barrier = pltpu.get_barrier_semaphore()

    @pl.loop(1, N_CTX)
    def _(d):
        pl.semaphore_signal(barrier, inc=1, device_id=(me, (c + d) % N_CTX), device_id_type=MESH)

    @pl.loop(0, wins)
    def _(i):
        w, _ = window(i)

        @pl.when(w != me)
        def _():
            pl.semaphore_signal(barrier, inc=1, device_id=(w, c), device_id_type=MESH)

    yf_all[c] = yf_ref[...]
    gf_all[c] = gf_ref[...]
    gs_grp[j] = gs_ref[...]
    ys_grp[j] = ys_ref[...]
    wg_all[j] = wg[0]
    wu_all[j] = wu[0]
    wd_all[j] = wd[0]
    wl_all[c] = wl[...]

    @pl.when(active)
    def _():
        pl.semaphore_wait(barrier, n_exp - 1 + N_CTX - 1)

    @pl.when(inactive)
    def _():
        pl.semaphore_wait(barrier, N_CTX - 1)


    def send_first(to):
        remote(yf_all.at[c], yf_all.at[c], yf_s, yf_r, me, to).start()

    def first_here(who):
        pl.when(who)(lambda: wait_bytes(yf_all.at[pl.ds(0, 7)], yf_r))

    for to in acts:
        pl.when(to != c)(functools.partial(send_first, to))
    owed["first, handler"] = functools.partial(first_here, active)

    @pl.when(inactive)
    def _():
        remote(gs_grp.at[j], gs_grp.at[j], grp_s.at[0], grp_r.at[0], me, act).start()
        remote(ys_grp.at[j], ys_grp.at[j], grp_s.at[1], grp_r.at[1], me, act).start()

    def group_sent(ref, n):
        pl.when(inactive)(lambda: wait_bytes(ref.at[0], grp_s.at[n]))

    def group_here(ref, n):
        pl.when(active)(lambda: wait_bytes(ref.at[pl.ds(0, 3)], grp_r.at[n]))

    for n, (name, ref) in enumerate((("gs", gs_grp), ("ys", ys_grp))):
        owed[name + " sent"] = functools.partial(group_sent, ref, n)
        owed[name] = functools.partial(group_here, ref, n)

    w_alls = (wg_all, wu_all, wd_all)
    j_nbr = nbr % 4

    for n, w_all in enumerate(w_alls):
        remote(w_all.at[j], w_all.at[j], w_s.at[n, 0], w_r.at[n, 0], me, nbr).start()
        remote(w_all.at[j], w_all.at[j], w_s.at[n, 1], w_r.at[n, 1], me, mate).start()
        for i in range(2):
            owe(f"w{n}{i} sent", w_all.at[0], w_s.at[n, i])
            owe(f"w{n}{i}", w_all.at[0], w_r.at[n, i])

    @pl.loop(1, 4)
    def _(d):
        remote(wl_all.at[c], wl_all.at[c], wl_s.at[0], wl_r.at[0], me, (c + 2 * d) % N_CTX).start()

    remote(wl_all.at[c], wl_all.at[c], wl_s.at[0], wl_r.at[1], me, mate).start()
    owe("wl sent", wl_all.at[pl.ds(0, 4)], wl_s.at[0])
    owe("wl, far", wl_all.at[pl.ds(0, 3)], wl_r.at[0])
    owe("wl, mate", wl_all.at[0], wl_r.at[1])

    def forward(n):
        w_all = w_alls[n]
        settle(f"w{n}0")
        remote(w_all.at[j_nbr], w_all.at[j_nbr], w_s.at[n, 2], w_r.at[n, 2], me, mate).start()
        owe(f"w{n}2 sent", w_all.at[0], w_s.at[n, 2])
        owe(f"w{n}2", w_all.at[0], w_r.at[n, 2])

    def have(n):
        settle(f"w{n}1", f"w{n}2")

    tokens = yf_ref.shape[0]
    slots = n_exp * cap

    def stat_rows(stat):
        row = jnp.broadcast_to(stat, (tokens, 128)).T[0:8]
        high = row.astype(BF16).astype(F32)
        return jnp.concatenate([high, row - high], axis=0).astype(BF16)

    def stat_column(arrived, at):
        row = arrived[at : at + 1] + arrived[at + 8 : at + 9]
        return jnp.broadcast_to(row, (tokens, tokens)).T

    def one_hot(hit):
        return jnp.where(hit, 1.0, 0.0).astype(BF16)

    def routes():
        expert = iota((n_exp, tokens), 0)
        named = jnp.zeros((n_exp, tokens), F32)
        gates = jnp.zeros((n_exp, tokens), F32)
        for t in range(ids_ref.shape[0]):
            hit = ids_ref[t : t + 1, :] == expert
            named = jnp.where(hit, 1.0, named)
            gates = jnp.where(hit, gate_ref[t : t + 1, :].astype(F32), gates)
        before = one_hot(iota((tokens, tokens), 0) < iota((tokens, tokens), 1))
        rank = dot_nn(named.astype(BF16), before)
        code = jnp.where(named > 0.5, rank, 255.0).astype(BF16)
        high = jnp.floor(gates * (1.0 / 256.0))
        return code, high.astype(BF16), (gates - 256.0 * high).astype(BF16)

    @pl.when(active)
    def _():
        code, _, _ = routes()
        spread = one_hot(iota((slots, n_exp), 0) // cap == iota((slots, n_exp), 1))
        place = (iota((slots, tokens), 0) % cap).astype(F32)
        chooser[...] = one_hot(dot_nn(spread, code) == place)

    settle("first, handler")

    def dispatch(n, send, arrive):
        @pl.loop(1, n_exp)
        def _(i):
            e = shifted(n_exp - i)
            remote(send.at[e], arrive.at[p, my_wi], disp_s.at[n], disp_r.at[n], e, c).start()

        pltpu.make_async_copy(send.at[me], arrive.at[p, my_wi], disp_r.at[n]).start()

    def dispatch_sent(ref, n):
        pl.when(active)(lambda: wait_bytes(ref.at[pl.ds(0, n_exp - 1)], disp_s.at[n]))

    @pl.when(active)
    def _():
        r = scale_of(wide(yf_all, 8).astype(F32))
        normed = jnp.concatenate([yf_all[4 * p + i] for i in range(4)], axis=1).astype(F32)
        normed = (normed * r * g_moe[:, half]).astype(BF16)
        rows_send[...] = dot_nn(chooser[...], normed).astype(BF16).reshape(n_exp, cap, 512)
        dispatch(0, rows_send, rows_in)

    owed["rows sent"] = functools.partial(dispatch_sent, rows_send, 0)
    owe("rows", rows_in.at[0], disp_r.at[0])
    @pl.when(active)
    def _():
        code, high, low = routes()
        spread = one_hot(iota((n_exp, slots), 1) // cap == iota((n_exp, slots), 0))
        place = (iota((tokens, slots), 1) % cap).astype(F32)
        taken = dot_tn(code, spread) == place
        for part, (levels, unit) in enumerate(((high, 256.0), (low, 65536.0))):
            comb[part * tokens : (part + 1) * tokens] = jnp.where(
                taken, dot_tn(levels, spread) * (1.0 / unit), 0.0
            ).astype(BF16)

    @pl.loop(1, N_CTX)
    def _(d):
        to = (c + d) % N_CTX
        pl.when((to != acts[0]) & (to != acts[1]))(functools.partial(send_first, to))
        remote(gf_all.at[c], gf_all.at[c], gf_s, gf_r, me, to).start()

    owe("first sent", yf_all.at[pl.ds(0, 7)], yf_s)
    owed["first"] = functools.partial(first_here, inactive)
    owe("gf sent", gf_all.at[pl.ds(0, 7)], gf_s)
    owe("gf", gf_all.at[pl.ds(0, 7)], gf_r)
    settle("rows")

    def to_cross(n, src, dst):
        remote(src, dst, cross_s.at[n], cross_r.at[n], me, cross).start()
        owe(f"cross{n} sent", src, cross_s.at[n])
        owe(f"cross{n}", dst, cross_r.at[n])

    to_cross(0, rows_in.at[p], rows_in.at[p])
    settle("gs")

    @pl.when(active)
    def _():
        grads_send[...] = dot_nn(chooser[...], wide(gs_grp, 4)).astype(BF16).reshape(n_exp, cap, 512)
        dispatch(1, grads_send, grads_in)

    owed["grads sent"] = functools.partial(dispatch_sent, grads_send, 1)
    owe("grads", grads_in.at[0], disp_r.at[1])

    for n in range(3):
        forward(n)
    settle("wl, far")

    @pl.loop(1, 4)
    def _(d):
        slot = (c + 2 * d) % N_CTX
        remote(wl_all.at[slot], wl_all.at[slot], wl_s.at[1], wl_r.at[2], me, mate).start()

    owe("wl forwarded", wl_all.at[pl.ds(0, 3)], wl_s.at[1])
    owe("wl, mate's far", wl_all.at[pl.ds(0, 3)], wl_r.at[2])

    settle("cross0")
    n_rows = wins * cap
    hid = 4 * wg.shape[1]

    def both(ref):
        return jnp.concatenate([ref[0].reshape(n_rows, 512), ref[1].reshape(n_rows, 512)], axis=1)

    def weight(ref):
        return ref[...].reshape(hid, 1024)

    def weight_half(ref, cols):
        return ref[:, :, cols].reshape(hid, 512)

    have(0)
    rows = both(rows_in)
    gate_proj = dot_nt(rows, weight(wg_all))
    have(1)
    up_proj = dot_nt(rows, weight(wu_all))
    gate_keep[...] = gate_proj
    up_keep[...] = up_proj
    hidden = (gate_proj * jax.nn.sigmoid(gate_proj) * up_proj).astype(BF16)
    have(2)
    xo_send[...] = dot_nn(hidden, weight_half(wd_all, other)).astype(BF16)
    to_cross(1, xo_send, xo_recv)
    own_out = dot_nn(hidden, weight_half(wd_all, half))

    settle("grads")
    to_cross(2, grads_in.at[p], grads_in.at[p])

    def give_back(ret, back, n):
        @pl.loop(0, wins)
        def _(i):
            w, wi = window(i)

            @pl.when(w != me)
            def _():
                remote(ret.at[wi], back.at[me], ret_s.at[n], ret_r.at[n], w, c).start()

        @pl.when(active)
        def _():
            pltpu.make_async_copy(ret.at[my_wi], back.at[me], ret_r.at[n]).start()

        def sent():
            pl.when(inactive)(lambda: wait_bytes(ret, ret_s.at[n]))
            if wins > 1:
                pl.when(active)(lambda: wait_bytes(ret.at[pl.ds(0, wins - 1)], ret_s.at[n]))

        owed[f"ret{n} sent"] = sent
        owed[f"ret{n}"] = lambda: pl.when(active)(lambda: wait_bytes(back, ret_r.at[n]))

    settle("cross1")
    out_ret[...] = (own_out + xo_recv[...].astype(F32)).astype(BF16).reshape(wins, cap, 512)
    give_back(out_ret, out_back, 0)

    for i in range(2):
        wo_split[i] = wo[:, 512 * i : 512 * i + 512]
    wo_all[c] = wo_split[p]

    def send_wo(i):
        remote(wo_split.at[i], wo_all.at[c], wo_s, wo_r, me, acts[i]).start()

    def wo_sent():
        pl.when(inactive)(lambda: wait_bytes(wo_split, wo_s))
        pl.when(active)(lambda: wait_bytes(wo_split.at[0], wo_s))

    for i in range(2):
        pl.when(acts[i] != c)(functools.partial(send_wo, i))
    owed["wo sent"] = wo_sent
    owed["wo"] = lambda: pl.when(active)(lambda: wait_bytes(wo_all.at[pl.ds(0, 7)], wo_r))
    settle("cross2")
    grad_hidden = dot_nt(both(grads_in), weight(wd_all))
    gate_proj = gate_keep[...]
    sig = jax.nn.sigmoid(gate_proj)
    grad_gate = (grad_hidden * up_keep[...] * sig * (1.0 + gate_proj * (1.0 - sig))).astype(BF16)
    grad_up = (grad_hidden * gate_proj * sig).astype(BF16)
    xb_send[...] = (
        dot_nn(grad_gate, weight_half(wg_all, other)) + dot_nn(grad_up, weight_half(wu_all, other))
    ).astype(BF16)
    to_cross(3, xb_send, xb_recv)
    own_back = dot_nn(grad_gate, weight_half(wg_all, half)) + dot_nn(grad_up, weight_half(wu_all, half))
    settle("cross3")
    bk_ret[...] = (own_back + xb_recv[...].astype(F32)).astype(BF16).reshape(wins, cap, 512)
    give_back(bk_ret, bk_back, 1)
    def combined(back):
        sums = dot_nn(comb[...], back[...].reshape(n_exp * cap, 512))
        return sums[0:tokens] + sums[tokens : 2 * tokens]

    settle("ys", "ret0")

    @pl.when(active)
    def _():
        sec[p] = (wide(ys_grp, 4).astype(F32) - combined(out_back)).astype(BF16)

    direct = k == qk

    @pl.when(active)
    def _():
        @pl.loop(1, 4)
        def _(d):
            remote(sec.at[p], sec.at[p], sec_s.at[0], sec_r.at[p], me, (c + 2 * d) % N_CTX).start()

    @pl.when(direct)
    def _():
        for h in range(2):
            pl.when(inactive | (p != h))(functools.partial(wait_bytes, sec.at[h], sec_r.at[h]))
            remote(sec.at[h], sec.at[h], sec_s.at[1], sec_r.at[h], me, mate).start()

    @pl.when(jnp.logical_not(direct))
    def _():
        for h in range(2):
            wait_bytes(sec.at[h], sec_r.at[h])

    def second_sent():
        pl.when(active)(lambda: wait_bytes(sec.at[pl.ds(0, 3)], sec_s.at[0]))
        pl.when(direct)(lambda: wait_bytes(sec.at[pl.ds(0, 2)], sec_s.at[1]))

    owed["sec sent"] = second_sent
    own_lanes = pl.ds(pl.multiple_of(j * 128, 128), 128)
    second_out[...] = sec[p, :, own_lanes]

    second = jnp.concatenate([sec[0], sec[1]], axis=1).astype(F32)
    r_second = scale_of(second)
    attn_in = (second * r_second * g_attn[...]).astype(BF16)
    queries = dot_nn(attn_in, wq[...]).astype(BF16)
    wl2 = jnp.concatenate([wl[...], wl[...]], axis=0)
    lane = iota((tokens, 128), 1)
    mine = lane // 64 == k
    lat_all[c] = jnp.where(mine, dot_nt(attn_in, wl2), 0.0).astype(BF16)

    @pl.loop(1, N_CTX)
    def _(d):
        remote(lat_all.at[c], lat_all.at[c], lat_s, lat_r, me, (c + d) % N_CTX).start()

    owe("lat sent", lat_all.at[pl.ds(0, 7)], lat_s)
    owe("lat", lat_all.at[pl.ds(0, 7)], lat_r)
    settle("lat")
    latent = jnp.concatenate(
        [lat_all[2 * i].astype(F32) + lat_all[2 * i + 1].astype(F32) for i in range(4)], axis=1
    )
    r_latent = scale_of(latent)
    latent_norm = (latent * r_latent * g_lat[...]).astype(BF16)
    keys = dot_nn(latent_norm, wk[...]).astype(BF16)
    values = dot_nn(latent_norm, wv[...]).astype(BF16)
    factor = 1.0 / math.sqrt(128.0)
    bounded = jnp.tanh(dot_nt(queries, keys) * (factor / LIMIT))
    allowed = iota((tokens, tokens), 1) <= iota((tokens, tokens), 0)
    weights = jnp.where(allowed, jnp.exp(LIMIT * bounded), 0.0)
    probs = weights / jnp.sum(weights, axis=-1, keepdims=True)
    probs_low = probs.astype(BF16)
    mixed = dot_nn(probs_low, values).astype(BF16)
    attn_part = dot_nn(mixed, wo[...]).astype(BF16)
    for i in range(N_CTX):
        ao_send[i] = attn_part[:, 128 * i : 128 * i + 128]
    ao_recv[c] = ao_send[c]

    @pl.loop(1, N_CTX)
    def _(d):
        to = (c + d) % N_CTX
        remote(ao_send.at[to], ao_recv.at[c], ao_s, ao_r, me, to).start()

    owe("ao sent", ao_recv.at[pl.ds(0, 7)], ao_s)
    owe("ao", ao_recv.at[pl.ds(0, 7)], ao_r)
    settle("first", "gf")
    first = wide(yf_all, 8).astype(F32)
    r_first = scale_of(first)
    turned = dot_nt((first * (r_first * r_first * r_first)).astype(BF16), wo[...])

    settle("wl, mate", "wl, mate's far")
    own_cols = pl.ds(pl.multiple_of(c * 128, 128), 128)
    latent_cube = (latent * (r_latent * r_latent * r_latent)).astype(BF16)
    project = wl_all[...].reshape(512, 1024)
    own_turn = dot_nn(latent_cube, wl_all[:, :, own_cols].reshape(512, 128))
    turn_stat = jnp.sum(g_attn[...] * dot_nn(latent_cube, project) * second, axis=-1, keepdims=True)

    settle("ret1", "wo")

    @pl.when(active)
    def _():
        grad = combined(bk_back)
        lifted = g_moe[:, half] * grad
        own_first = jnp.concatenate([yf_all[4 * p + i] for i in range(4)], axis=1).astype(F32)
        own_grad = jnp.concatenate([gf_all[4 * p + i] for i in range(4)], axis=1).astype(F32)
        part = dot_nt((own_grad + r_first * lifted).astype(BF16), wo_all[...].reshape(1024, 512))
        inner_rows = stat_rows(jnp.sum(lifted * own_first, axis=-1, keepdims=True))
        for i in range(N_CTX):
            gp_send[i, 0:tokens] = part[:, 128 * i : 128 * i + 128].astype(BF16)
            gp_send[i, tokens : tokens + 16] = inner_rows
        gp_recv[p] = gp_send[c]

        @pl.loop(1, N_CTX)
        def _(d):
            to = (c + d) % N_CTX
            remote(gp_send.at[to], gp_recv.at[p], gp_s, gp_r.at[p], me, to).start()

        for i in range(4):
            us[i] = grad[:, 128 * i : 128 * i + 128].astype(BF16)
        us_in[...] = us[j]

        @pl.loop(1, 4)
        def _(d):
            to = (j + d) % 4
            remote(us.at[to], us_in, us_s, us_r, me, 4 * p + to).start()

    def parts_sent():
        @pl.when(active)
        def _():
            wait_bytes(gp_send.at[pl.ds(0, 7)], gp_s)
            wait_bytes(us.at[pl.ds(0, 3)], us_s)

    def parts_here():
        pl.when(inactive)(lambda: wait_bytes(gp_recv.at[0], gp_r.at[p]))
        wait_bytes(gp_recv.at[0], gp_r.at[1 - p])

    owed["parts sent"] = parts_sent
    owed["parts"] = parts_here
    owed["us"] = lambda: pl.when(inactive)(lambda: wait_bytes(us_in, us_r))

    settle("ao")
    attn_out = ao_recv[0].astype(F32)
    for i in range(1, N_CTX):
        attn_out = attn_out + ao_recv[i].astype(F32)
    first_out[...] = (yf_ref[...].astype(F32) - attn_out).astype(BF16)

    settle("parts")
    arrived = gp_recv[0].astype(F32) + gp_recv[1].astype(F32)
    first_inner = stat_column(arrived, tokens) * (1.0 / 1024.0)
    grad_mixed = (arrived[0:tokens] - first_inner * turned).astype(BF16)
    grad_probs = dot_nt(grad_mixed, values)
    row_delta = jnp.sum(probs * grad_probs, axis=-1, keepdims=True)
    grad_scores = (probs * (grad_probs - row_delta) * (1.0 - bounded * bounded) * factor).astype(BF16)
    grad_keys = dot_tn(grad_scores, queries).astype(BF16)
    grad_values = dot_tn(probs_low, grad_mixed).astype(BF16)
    lat_part = dot_nt(grad_keys, wk[...]) + dot_nt(grad_values, wv[...])
    lifted = g_lat[...] * lat_part
    grad_queries = dot_nn(grad_scores, keys).astype(BF16)
    input_part = dot_nt(grad_queries, wq[...]) + dot_nn((r_latent * lifted).astype(BF16), project)
    lat_stat = stat_rows(jnp.sum(lifted * latent, axis=-1, keepdims=True))
    stat = jnp.sum(g_attn[...] * input_part * second, axis=-1, keepdims=True)
    in_stat = stat_rows(stat)
    for i in range(N_CTX):
        ia_send[i, 0:tokens] = input_part[:, 128 * i : 128 * i + 128].astype(BF16)
        ia_send[i, tokens : tokens + 16] = in_stat
        ia_send[i, tokens + 16 : tokens + 32] = lat_stat
    ia_recv[c] = ia_send[c]

    @pl.loop(1, N_CTX)
    def _(d):
        to = (c + d) % N_CTX
        remote(ia_send.at[to], ia_recv.at[c], ia_s, ia_r, me, to).start()

    settle("us")
    moe_gain = g_moe[:, own_cols]
    grad_first = r_first * (moe_gain * us_in[...].astype(F32)) - yf_ref[...].astype(F32) * (
        r_first * r_first * r_first
    ) * first_inner
    gfirst_out[...] = (gf_ref[...].astype(F32) + grad_first).astype(BF16)
    owe("ia sent", ia_recv.at[pl.ds(0, 7)], ia_s)
    owe("ia", ia_recv.at[pl.ds(0, 7)], ia_r)
    settle("ia")
    arrived = ia_recv[0].astype(F32)
    for i in range(1, N_CTX):
        arrived = arrived + ia_recv[i].astype(F32)
    lat_inner = stat_column(arrived, tokens + 16) * (1.0 / 512.0)
    in_inner = (stat_column(arrived, tokens) - lat_inner * turn_stat) * (1.0 / 1024.0)
    own_gain = g_attn[:, own_cols]
    own_second = sec[p, :, own_lanes].astype(F32)
    grad_in = r_second * (own_gain * (arrived[0:tokens] - lat_inner * own_turn)) - own_second * (
        r_second * r_second * r_second
    ) * in_inner
    gsecond_out[...] = (gs_ref[...].astype(F32) + grad_in).astype(BF16)

    settle(*owed)


def hand_over(*refs):
    for i in range(4):
        refs[4 + i][...] = refs[i][...]


def local(n_x, n_z, cap, *args):
    (yf, ys, gf, gs, ids, gate, ga, gl, gmo, wq, wl, wk, wv, wo, wg, wu, wd) = args
    tokens = yf.shape[0]
    n_exp = n_x * n_z
    wins = n_exp // 4
    hid = wg.shape[2]
    block = (tokens, 128)
    vmem = lambda *s: pltpu.VMEM(s, BF16)
    dma = pltpu.SemaphoreType.DMA
    one = dma(())
    out = jax.ShapeDtypeStruct(block, BF16)
    spec = pl.BlockSpec(memory_space=pltpu.VMEM)
    results = pl.pallas_call(
        functools.partial(kernel, n_x, n_z, cap),
        out_shape=(out,) * 4,
        in_specs=[spec] * 17,
        out_specs=(spec,) * 4,
        scratch_shapes=[
            vmem(8, *block),
            vmem(8, *block),
            vmem(4, *block),
            vmem(4, *block),
            vmem(4, hid, 1024),
            vmem(4, hid, 1024),
            vmem(4, hid, 1024),
            vmem(n_exp * cap, tokens),
            vmem(2 * tokens, n_exp * cap),
            vmem(n_exp, cap, 512),
            vmem(n_exp, cap, 512),
            vmem(2, wins, cap, 512),
            vmem(2, wins, cap, 512),
            pltpu.VMEM((wins * cap, 4 * hid), F32),
            pltpu.VMEM((wins * cap, 4 * hid), F32),
            vmem(wins * cap, 512),
            vmem(wins * cap, 512),
            vmem(wins, cap, 512),
            vmem(n_exp, cap, 512),
            vmem(wins * cap, 512),
            vmem(wins * cap, 512),
            vmem(wins, cap, 512),
            vmem(n_exp, cap, 512),
            vmem(8, tokens, 512),
            vmem(2, 128, 512),
            vmem(8, 128, 512),
            vmem(8, tokens + 16, 128),
            vmem(2, tokens + 16, 128),
            vmem(4, *block),
            vmem(*block),
            vmem(8, *block),
            vmem(8, *block),
            vmem(8, *block),
            vmem(8, 64, 1024),
            vmem(8, tokens + 32, 128),
            vmem(8, tokens + 32, 128),
            one,
            one,
            one,
            one,
            dma((2,)),
            dma((2,)),
            dma((3, 3)),
            dma((3, 3)),
            dma((2,)),
            dma((2,)),
            dma((4,)),
            dma((4,)),
            dma((2,)),
            dma((2,)),
            dma((2,)),
            dma((2,)),
            one,
            one,
            one,
            dma((2,)),
            one,
            one,
            one,
            one,
            one,
            one,
            dma((2,)),
            dma((3,)),
            one,
            one,
        ],
        compiler_params=pltpu.CompilerParams(
            collective_id=0, has_side_effects=True, vmem_limit_bytes=56 * 1024 * 1024
        ),
    )(
        *(yf, ys, gf, gs, ids.T, gate.T),
        *(g.reshape(1, -1) for g in (ga, gl, gmo)),
        *(wq, wl.T, wk, wv, wo),
        *(jnp.swapaxes(w, 1, 2) for w in (wg, wu)),
        wd,
    )
    return pl.pallas_call(
        hand_over, out_shape=(out,) * 4, in_specs=[spec] * 4, out_specs=(spec,) * 4
    )(*results)


def solution(mesh, n_x=4, n_z=16, cap=CAP):
    rows = P("exp", "ctx")
    placed = (
        (rows,) * 4
        + (P("exp", None),) * 2
        + (P(),) * 3
        + (P(None, "ctx"),) * 4
        + (P("ctx", None), P("exp", None, "ctx"), P("exp", None, "ctx"), P("exp", "ctx", None))
    )
    return jax.shard_map(
        functools.partial(local, n_x, n_z, cap),
        mesh=mesh,
        in_specs=placed,
        out_specs=(rows,) * 4,
        check_vma=False,
    )
```
